512 devices in a mesh: section: 16 (over x, z_lo), tp: 4 (over z_hi, core), dp: 8 (over y).
Axes of the slice: x: 4, y: 8, z: 8 (z_hi: 2, z_lo: 4; z = z_hi * 4 + z_lo), core: 2. Of those that a mesh axis runs over, the one named last changes fastest.
Arguments:
- inputs: bfloat16 [4, 384, 7168], P(None, 'dp', 'tp'), may hold values from -6 to 6
- norm_gain: float32 [16, 7168], P('section', 'tp'), may hold values from 0.25 to 1.75
- norm_bias: float32 [16, 7168], P('section', 'tp'), may hold values from -3 to 3
- mix: bfloat16 [16, 56, 128, 128], P('section', 'tp'), may hold values from -0.5 to 0.5
Outputs:
- gain_grad: float32 [16, 7168], P('section', 'tp')
- bias_grad: float32 [16, 7168], P('section', 'tp')
- mix_grad: float32 [16, 56, 128, 128], P('section', 'tp', 'dp')
The draws below stay inside these ranges and needn't reach their ends.
All inputs are finite; a program needn't handle non-finite values.
Results may differ from the reference program's by a relative error of at most 0.0011.
Values may be sent and summed in bfloat16 or wider, within the bound.
A program may use at most 64 MiB of HBM per device.

```python
import math
import jax
import jax.numpy as jnp
from jax import lax

D = 7168
HEADS = 56
HS = 128
MB = 4
TOKENS = 384
PARAMS = 14909440
N_SECTION = 16


def block_levels(stream_key, dims, cuts, smallest, largest):
    level = 1.0
    for dim, parts in cuts:
        steps = jax.random.uniform(jax.random.fold_in(jax.random.fold_in(stream_key, 6), dim), (parts,), jnp.float32, smallest / len(cuts), largest / len(cuts))
        level = level * jnp.repeat(jnp.exp(steps), dims[dim] // parts).reshape((-1,) + (1,) * (len(dims) - 1 - dim))
    return level


def normal_values(key, extent, scale, most, shards=(), dtype=jnp.bfloat16):
    drawn = scale * jax.random.normal(key, extent, jnp.float32)
    if shards:
        drawn = drawn * block_levels(key, extent, shards, -0.22, 0.18)
    return jnp.clip(drawn, -most, most).astype(dtype)


def setup_inputs(seed: int = 0) -> dict:
    key_list = jax.random.split(jax.random.key(seed), 5)
    inputs = normal_values(key_list[0], (MB, TOKENS, D), 1.0, 6.0, ((1, 8), (2, 4)))
    norm_gain = jnp.clip(1.0 + 0.15 * jax.random.normal(key_list[1], (N_SECTION, D), jnp.float32), 0.25, 1.75)
    norm_bias = normal_values(key_list[2], (N_SECTION, D), 0.5, 3.0, ((0, 16), (1, 4)), jnp.float32)
    mix = normal_values(key_list[3], (N_SECTION, HEADS, HS, HS), HS ** -0.5, 0.5, ((0, 16), (1, 4)))
    return {"inputs": inputs, "norm_gain": norm_gain, "norm_bias": norm_bias, "mix": mix}


EPSILON = 1e-05
GRAD_EPS = 1e-06
GELU_K = math.sqrt(2.0 / math.pi)
GELU_C = 0.044715

def gelu_tanh(value):
    return 0.5 * value * (1.0 + jnp.tanh(GELU_K * (value + GELU_C * value * value * value)))

def gelu_slope(value):
    tangent = jnp.tanh(GELU_K * (value + GELU_C * value * value * value))
    return 0.5 * (1.0 + tangent) + 0.5 * value * (1.0 - tangent * tangent) * GELU_K * (1.0 + 3.0 * GELU_C * value * value)

def normalize(split_in):
    mean_val = lax.optimization_barrier(jnp.mean(split_in, axis=-1, keepdims=True))
    centred = split_in - mean_val
    variance = lax.optimization_barrier(jnp.mean(centred * centred, axis=-1, keepdims=True))
    inv_std = jax.lax.rsqrt(variance + EPSILON)
    return (centred * inv_std, inv_std)

def layer_forward(block_in, gain_row, bias_row, weights):
    row_count = block_in.shape[0]
    wide_in = block_in.astype(jnp.float32)
    normed, inv_std = normalize(wide_in.reshape(row_count, HEADS, HS))
    normed = normed.reshape(row_count, D)
    activated = gelu_tanh(normed * gain_row + bias_row).astype(jnp.bfloat16)
    split_act = activated.astype(jnp.float32).reshape(row_count, HEADS, HS)
    mixed = jnp.einsum('rhk,hkj->rhj', split_act, weights.astype(jnp.float32)).reshape(row_count, D)
    return (wide_in + mixed).astype(jnp.bfloat16)

def layer_backward(block_in, grad_out, gain_row, bias_row, weights):
    row_count = block_in.shape[0]
    wide_in = block_in.astype(jnp.float32)
    normed3, inv_std = normalize(wide_in.reshape(row_count, HEADS, HS))
    normed = normed3.reshape(row_count, D)
    pre_act = normed * gain_row + bias_row
    activated = gelu_tanh(pre_act).astype(jnp.bfloat16)
    split_grad = grad_out.astype(jnp.float32).reshape(row_count, HEADS, HS)
    grad_act = jnp.einsum('rhj,hkj->rhk', split_grad, weights.astype(jnp.float32)).reshape(row_count, D)
    grad_pre = grad_act * gelu_slope(pre_act)
    grad_norm = (grad_pre * gain_row).reshape(row_count, HEADS, HS)
    grad_centred = inv_std * (grad_norm - lax.optimization_barrier(jnp.mean(grad_norm, axis=-1, keepdims=True)) - normed3 * lax.optimization_barrier(jnp.mean(grad_norm * normed3, axis=-1, keepdims=True)))
    grad_in = (grad_out.astype(jnp.float32) + grad_centred.reshape(row_count, D)).astype(jnp.bfloat16)
    split_act = activated.astype(jnp.float32).reshape(row_count, HEADS, HS)
    mix_part = jnp.einsum('rhk,rhj->hkj', split_act, split_grad)
    return (grad_in, lax.optimization_barrier(jnp.sum(grad_pre * normed, axis=0)), lax.optimization_barrier(jnp.sum(grad_pre, axis=0)), mix_part)

def reference(inputs, norm_gain, norm_bias, mix):
    loss_scale = 1.0 / math.sqrt(MB * TOKENS)
    gain_list = [jnp.zeros((D,), jnp.float32) for index in range(N_SECTION)]
    bias_list = [jnp.zeros((D,), jnp.float32) for index in range(N_SECTION)]
    mix_list = [jnp.zeros((HEADS, HS, HS), jnp.float32) for index in range(N_SECTION)]
    for micro_batch in range(MB):
        current = inputs[micro_batch]
        saved = []
        for section_index in range(N_SECTION):
            saved.append(current)
            current = layer_forward(current, norm_gain[section_index], norm_bias[section_index], mix[section_index])
        grad_out = (current.astype(jnp.float32) * loss_scale).astype(jnp.bfloat16)
        for section_index in range(N_SECTION - 1, -1, -1):
            grad_in, gain_part, bias_part, mix_part = layer_backward(saved[section_index], grad_out, norm_gain[section_index], norm_bias[section_index], mix[section_index])
            gain_list[section_index] = gain_list[section_index] + gain_part
            bias_list[section_index] = bias_list[section_index] + bias_part
            mix_list[section_index] = mix_list[section_index] + mix_part
            grad_out = grad_in
    raw_gain = jnp.stack(gain_list)
    raw_bias = jnp.stack(bias_list)
    raw_mix = jnp.stack(mix_list)
    total = jnp.sum(raw_gain * raw_gain) + jnp.sum(raw_bias * raw_bias) + jnp.sum(raw_mix * raw_mix)
    scale = jax.lax.rsqrt(total / PARAMS + GRAD_EPS)
    return (raw_gain * scale, raw_bias * scale, raw_mix * scale)
```

```python
import functools
import math

import jax
import jax.numpy as jnp
from jax import lax
from jax.experimental import pallas as pl
from jax.experimental.pallas import tpu as pltpu
from jax.sharding import PartitionSpec as P

EPSILON = 1e-05
GRAD_EPS = 1e-06
GELU_K = math.sqrt(2.0 / math.pi)
GELU_C = 0.044715


def forward_layer(wide, gain, bias, weights):
    mean = jnp.mean(wide, axis=-1, keepdims=True)
    centred = wide - mean
    inv_std = lax.rsqrt(jnp.mean(centred * centred, axis=-1, keepdims=True) + EPSILON)
    normed = centred * inv_std
    pre = normed * gain + bias
    square = pre * pre
    tangent = jnp.tanh(pre * (GELU_K + (GELU_K * GELU_C) * square))
    half = 0.5 + 0.5 * tangent
    act = pre * half
    slope = half + act * (1.0 - tangent) * (GELU_K + (3.0 * GELU_K * GELU_C) * square)
    act = act.astype(jnp.bfloat16)
    mixed = jnp.dot(act, weights, preferred_element_type=jnp.float32)
    return (wide + mixed).astype(jnp.bfloat16), normed, inv_std, act, slope


def backward_layer(grad, normed, inv_std, act, slope, gain, weights):
    grad_act = lax.dot_general(
        grad, weights, (((1,), (1,)), ((), ())), preferred_element_type=jnp.float32
    )
    mix_part = lax.dot_general(
        act, grad, (((0,), (0,)), ((), ())), preferred_element_type=jnp.float32
    )
    grad_pre = grad_act * slope
    gain_term = grad_pre * normed
    grad_norm = grad_pre * gain
    first = jnp.mean(grad_norm, axis=-1, keepdims=True)
    second = jnp.mean(gain_term * gain, axis=-1, keepdims=True)
    grad_in = grad.astype(jnp.float32) + inv_std * (grad_norm - first - normed * second)
    gain_part = jnp.sum(gain_term, axis=0, keepdims=True)
    bias_part = jnp.sum(grad_pre, axis=0, keepdims=True)
    return grad_in.astype(jnp.bfloat16), mix_part, gain_part, bias_part


def stack_kernel(
    loss_scale, x_ref, params_ref, weights_ref, mix_ref, vec_ref, flow, normed_s, inv_s, act_s, slope_s
):
    layers = weights_ref.shape[0]
    flow[...] = x_ref[...]

    @pl.loop(0, layers)
    def _(layer):
        wide = flow[...].astype(jnp.float32)
        out, normed, inv_std, act, slope = forward_layer(
            wide, params_ref[layer, 0:1], params_ref[layer, 1:2], weights_ref[layer]
        )
        flow[...] = out
        normed_s[layer] = normed
        inv_s[layer] = jnp.broadcast_to(inv_std, normed.shape)
        act_s[layer] = act
        slope_s[layer] = slope

    flow[...] = (flow[...].astype(jnp.float32) * loss_scale).astype(jnp.bfloat16)

    @pl.loop(0, layers)
    def _(step):
        layer = layers - 1 - step
        grad_in, mix_part, gain_part, bias_part = backward_layer(
            flow[...],
            normed_s[layer],
            inv_s[layer],
            act_s[layer],
            slope_s[layer],
            params_ref[layer, 0:1],
            weights_ref[layer],
        )
        flow[...] = grad_in
        mix_ref[layer] = mix_part
        vec_ref[layer, 0:1] = gain_part
        vec_ref[layer, 1:2] = bias_part


def run_stack(x, params, weights, loss_scale):
    layers = weights.shape[0]
    rows, size = x.shape
    return pl.pallas_call(
        functools.partial(stack_kernel, loss_scale),
        out_shape=(
            jax.ShapeDtypeStruct((layers, size, size), jnp.float32),
            jax.ShapeDtypeStruct((layers, 2, size), jnp.float32),
        ),
        in_specs=[pl.BlockSpec(memory_space=pltpu.VMEM)] * 3,
        out_specs=[pl.BlockSpec(memory_space=pltpu.VMEM)] * 2,
        scratch_shapes=[
            pltpu.VMEM((rows, size), jnp.bfloat16),
            pltpu.VMEM((layers, rows, size), jnp.float32),
            pltpu.VMEM((layers, rows, size), jnp.float32),
            pltpu.VMEM((layers, rows, size), jnp.bfloat16),
            pltpu.VMEM((layers, rows, size), jnp.float32),
        ],
        compiler_params=pltpu.CompilerParams(vmem_limit_bytes=32 << 20),
        name="stack",
    )(x, params, weights)


def shards(inputs, norm_gain, norm_bias, mix):
    sections = lax.axis_size("section")
    me = lax.axis_index("section")
    batches, rows, features = inputs.shape
    heads, size = mix.shape[1], mix.shape[2]
    feature_total = features * lax.axis_size("tp")
    param_count = sections * (
        2 * feature_total + heads * lax.axis_size("tp") * size * size
    )
    loss_scale = 1.0 / math.sqrt(batches * rows * lax.axis_size("dp"))
    head = jnp.minimum(me, heads - 1)
    x = lax.dynamic_slice_in_dim(inputs, head * size, size, 2).reshape(batches * rows, size)
    params = jnp.stack([norm_gain.reshape(heads, size), norm_bias.reshape(heads, size)], 1)
    spare = sections - heads
    params = jnp.pad(params, ((0, spare), (0, 0), (0, 0)))
    weights = jnp.pad(mix[0], ((0, spare), (0, 0), (0, 0)))
    params = lax.all_to_all(params, "section", 0, 0, tiled=True)
    weights = lax.all_to_all(weights, "section", 0, 0, tiled=True)
    mix_part, vec_part = run_stack(x, params, weights, loss_scale)
    mix_sum = lax.psum_scatter(mix_part, "dp", scatter_dimension=1, tiled=True)
    vec_sum = lax.psum(vec_part, "dp")
    mix_sum = lax.all_to_all(mix_sum, "section", 0, 0, tiled=True)[:heads]
    vec_sum = lax.all_to_all(vec_sum, "section", 0, 0, tiled=True)[:heads]
    squares = jnp.sum(mix_sum * mix_sum) + jnp.sum(vec_sum * vec_sum) / lax.axis_size("dp")
    total = lax.psum(squares, ("section", "tp", "dp"))
    scale = lax.rsqrt(total / param_count + GRAD_EPS)
    vec_sum = vec_sum * scale
    return (
        vec_sum[:, 0].reshape(1, features),
        vec_sum[:, 1].reshape(1, features),
        (mix_sum * scale)[None],
    )


def solution(mesh):
    placed = (
        P(None, "dp", "tp"),
        P("section", "tp"),
        P("section", "tp"),
        P("section", "tp", None, None),
    )
    return jax.shard_map(
        shards,
        mesh=mesh,
        in_specs=placed,
        out_specs=(P("section", "tp"), P("section", "tp"), P("section", "tp", "dp", None)),
        check_vma=False,
    )
```

```python
import functools
import math

import jax
import jax.numpy as jnp
from jax import lax
from jax.experimental import pallas as pl
from jax.experimental.pallas import tpu as pltpu
from jax.sharding import PartitionSpec as P

EPSILON = 1e-05
GRAD_EPS = 1e-06
GELU_K = math.sqrt(2.0 / math.pi)
GELU_C = 0.044715


def forward_layer(wide, gain, bias, weights):
    mean = jnp.mean(wide, axis=-1, keepdims=True)
    centred = wide - mean
    inv_std = lax.rsqrt(jnp.mean(centred * centred, axis=-1, keepdims=True) + EPSILON)
    normed = centred * inv_std
    pre = normed * gain + bias
    square = pre * pre
    tangent = jnp.tanh(pre * (GELU_K + (GELU_K * GELU_C) * square))
    half = 0.5 + 0.5 * tangent
    act = pre * half
    slope = half + act * (1.0 - tangent) * (GELU_K + (3.0 * GELU_K * GELU_C) * square)
    act = act.astype(jnp.bfloat16)
    mixed = jnp.dot(act, weights, preferred_element_type=jnp.float32)
    return (wide + mixed).astype(jnp.bfloat16), normed, inv_std, act, slope


def backward_layer(grad, normed, inv_std, act, slope, gain, weights):
    grad_act = lax.dot_general(
        grad, weights, (((1,), (1,)), ((), ())), preferred_element_type=jnp.float32
    )
    mix_part = lax.dot_general(
        act, grad, (((0,), (0,)), ((), ())), preferred_element_type=jnp.float32
    )
    grad_pre = grad_act * slope
    gain_term = grad_pre * normed
    grad_norm = grad_pre * gain
    first = jnp.mean(grad_norm, axis=-1, keepdims=True)
    second = jnp.mean(gain_term * gain, axis=-1, keepdims=True)
    grad_in = grad.astype(jnp.float32) + inv_std * (grad_norm - first - normed * second)
    gain_part = jnp.sum(gain_term, axis=0, keepdims=True)
    bias_part = jnp.sum(grad_pre, axis=0, keepdims=True)
    return grad_in.astype(jnp.bfloat16), mix_part, gain_part, bias_part


MESH = pl.DeviceIdType.MESH
LAG = 3
AHEAD = 2


def relay_kernel(
    loss_scale,
    param_count,
    x_ref,
    gain_ref,
    bias_ref,
    mix_ref,
    raw_ref,
    scale_ref,
    x_in,
    stage,
    params,
    weights,
    flow,
    normed_s,
    inv_s,
    act_s,
    slope_s,
    part_mix,
    part_vec,
    out1,
    out2,
    out3,
    out4,
    in1,
    in2,
    in3,
    in4,
    square,
    all_dp,
    all_section,
    all_tp,
    x_sent,
    x_came,
    w_sent,
    w_came,
    p_sent,
    p_came,
    f_sent,
    f_came,
    sent1,
    sent2,
    sent3,
    sent4,
    came1,
    came2,
    came3,
    came4,
    dp_sent,
    dp_came,
    section_sent,
    section_came,
    tp_sent,
    tp_came,
):
    section, tp, dp = (lax.axis_index(name) for name in ("section", "tp", "dp"))
    layers = weights.shape[0]
    heads = mix_ref.shape[0]
    size = mix_ref.shape[1]
    half, quarter, eighth = size // 2, size // 4, size // 8
    pairs = lax.axis_size("dp") // 2
    core, high = lax.rem(tp, 2), lax.div(tp, 2)
    unit, z_bit = lax.div(section, 2), lax.rem(section, 2)
    pair, y_bit = lax.div(dp, 2), lax.rem(dp, 2)
    place = unit * pairs + pair
    kin = lax.div(place, heads)
    head = place - kin * heads
    active = place < 2 * heads
    owner_tp = high * 2 + kin
    part = core * 4 + y_bit * 2 + z_bit

    def remote(source, target, sent, came, **where):
        return pltpu.make_async_remote_copy(
            src_ref=source,
            dst_ref=target,
            send_sem=sent,
            recv_sem=came,
            device_id=where,
            device_id_type=MESH,
        )

    def send(is_here, source, target, sent, came, **where):
        @pl.when(is_here)
        def _():
            pltpu.make_async_copy(source, target, came).start()

        @pl.when(jnp.logical_not(is_here))
        def _():
            remote(source, target, sent, came, **where).start()

    def x_plan(other_pair):
        here = unit * pairs + other_pair
        goes = (lax.div(here, heads) == core) & (y_bit == z_bit)
        to_dp = other_pair * 2 + lax.rem(pair, 2)
        to_core = lax.div(dp, 4)
        mine = (to_dp == dp) & (to_core == core)
        return here - core * heads, goes, mine, to_dp, high * 2 + to_core

    for other_pair in range(pairs):
        item, goes, mine, to_dp, to_tp = x_plan(other_pair)

        @pl.when(goes)
        def _():
            columns = pl.ds(pl.multiple_of(item * size, size), size)
            send(
                mine,
                x_ref.at[:, :, columns],
                x_in,
                x_sent.at[other_pair],
                x_came,
                tp=to_tp,
                dp=to_dp,
            )

    for item in range(heads):
        columns = slice(item * size, (item + 1) * size)
        stage[item, 0:1] = gain_ref[0:1, columns]
        stage[item, 1:2] = bias_ref[0:1, columns]
    part_vec[...] = jnp.zeros_like(part_vec)
    square[...] = jnp.zeros_like(square)
    middle = lax.div(heads + pairs - 1 - pair, pairs)
    stop = lax.div(2 * heads + pairs - 1 - pair, pairs)
    low = jnp.where(core == 0, 0, middle)
    high_end = jnp.where(core == 0, middle, stop)

    @pl.loop(low, high_end)
    def _(to_unit):
        item = to_unit * pairs + pair - core * heads
        for bit in range(2):
            to_section = to_unit * 2 + bit
            for to_core in range(2):
                mine = (to_section == section) & (core == to_core)
                rows = pl.ds(to_core * half, half)
                to_tp = high * 2 + to_core
                send(
                    mine,
                    stage.at[item],
                    params.at[section],
                    p_sent.at[to_section, to_core],
                    p_came.at[section],
                    section=to_section,
                    tp=to_tp,
                )
                send(
                    mine,
                    mix_ref.at[item, rows],
                    weights.at[section, rows],
                    w_sent.at[to_section, to_core],
                    w_came.at[section],
                    section=to_section,
                    tp=to_tp,
                )

    sibling = high * 2 + 1 - core
    own_rows = pl.ds(pl.multiple_of(core * half, half), half)
    other_rows = pl.ds(pl.multiple_of((1 - core) * half, half), half)

    def forward_half(layer):
        own = weights.at[layer, own_rows]
        return remote(own, own, f_sent.at[layer], f_came.at[layer], tp=sibling)

    def pass_on(layer):
        own = weights.at[layer, own_rows]
        remote(own, own, w_sent.at[0, 0], w_came.at[layer], tp=sibling).wait_recv()
        forward_half(layer).start()

    def exchange1(layer):
        return remote(
            out1.at[layer], in1.at[layer], sent1.at[layer], came1.at[layer], tp=sibling
        )

    def exchange2(layer):
        return remote(
            out2.at[layer],
            in2.at[layer],
            sent2.at[layer],
            came2.at[layer],
            dp=pair * 2 + 1 - y_bit,
        )

    def exchange3(layer):
        return remote(
            out3.at[layer],
            in3.at[layer],
            sent3.at[layer],
            came3.at[layer],
            section=unit * 2 + 1 - z_bit,
        )

    def to_owner(layer):
        return remote(
            out4.at[layer],
            in4.at[head],
            sent4.at[layer],
            came4.at[head],
            section=layer,
            tp=owner_tp,
            dp=part,
        )

    def is_owner(layer):
        return (layer == section) & (owner_tp == tp) & (part == dp)

    def rows_of(ref, layer, start, count):
        return ref[layer, pl.ds(pl.multiple_of(start, 8), count)]

    @pl.when(active)
    def _():
        remote(x_in, x_in, x_sent.at[0], x_came, tp=sibling).wait_recv()
        flow[...] = x_in[...].reshape(flow.shape)
        for layer in range(AHEAD):
            pass_on(layer)

        @pl.loop(0, layers)
        def _(layer):
            @pl.when(layer + AHEAD < layers)
            def _():
                pass_on(layer + AHEAD)

            remote(
                stage.at[0], params.at[layer], p_sent.at[0, 0], p_came.at[layer], tp=sibling
            ).wait_recv()
            theirs = weights.at[layer, other_rows]
            remote(theirs, theirs, f_sent.at[layer], f_came.at[layer], tp=sibling).wait_recv()
            wide = flow[...].astype(jnp.float32)
            out, normed, inv_std, act, slope = forward_layer(
                wide, params[layer, 0:1], params[layer, 1:2], weights[layer]
            )
            flow[...] = out
            normed_s[layer] = normed
            inv_s[layer] = jnp.broadcast_to(inv_std, normed.shape)
            act_s[layer] = act
            slope_s[layer] = slope

        flow[...] = (flow[...].astype(jnp.float32) * loss_scale).astype(jnp.bfloat16)

        @pl.loop(0, layers + 3 * LAG)
        def _(tick):
            @pl.when(tick < layers)
            def _():
                layer = layers - 1 - tick
                grad_in, mix_part, gain_part, bias_part = backward_layer(
                    flow[...],
                    normed_s[layer],
                    inv_s[layer],
                    act_s[layer],
                    slope_s[layer],
                    params[layer, 0:1],
                    weights[layer],
                )
                flow[...] = grad_in
                part_mix[layer] = mix_part
                part_vec[layer, 0:1] = gain_part
                part_vec[layer, 1:2] = bias_part
                out1[layer, 0:half] = rows_of(part_mix, layer, (1 - core) * half, half)
                out1[layer, half:] = part_vec[layer]
                exchange1(layer).start()

            step2 = tick - LAG

            @pl.when((step2 >= 0) & (step2 < layers))
            def _():
                layer = layers - 1 - step2
                exchange1(layer).wait_recv()
                away = (1 - y_bit) * quarter
                out2[layer, 0:quarter] = rows_of(
                    part_mix, layer, core * half + away, quarter
                ) + rows_of(in1, layer, away, quarter)
                out2[layer, quarter:] = part_vec[layer] + in1[layer, half:]
                exchange2(layer).start()

            step3 = tick - 2 * LAG

            @pl.when((step3 >= 0) & (step3 < layers))
            def _():
                layer = layers - 1 - step3
                exchange2(layer).wait_recv()
                away = (1 - z_bit) * eighth
                out3[layer, 0:eighth] = (
                    rows_of(part_mix, layer, core * half + y_bit * quarter + away, eighth)
                    + rows_of(in1, layer, y_bit * quarter + away, eighth)
                ) + rows_of(in2, layer, away, eighth)
                out3[layer, eighth:] = (part_vec[layer] + in1[layer, half:]) + in2[
                    layer, quarter:
                ]
                exchange3(layer).start()

            step4 = tick - 3 * LAG

            @pl.when((step4 >= 0) & (step4 < layers))
            def _():
                layer = layers - 1 - step4
                exchange3(layer).wait_recv()
                mix_sum = (
                    (
                        rows_of(part_mix, layer, part * eighth, eighth)
                        + rows_of(in1, layer, y_bit * quarter + z_bit * eighth, eighth)
                    )
                    + rows_of(in2, layer, z_bit * eighth, eighth)
                ) + in3[layer, 0:eighth]
                vec_sum = (
                    (part_vec[layer] + in1[layer, half:]) + in2[layer, quarter:]
                ) + in3[layer, eighth:]
                out4[layer, 0:eighth] = mix_sum
                out4[layer, eighth:] = vec_sum

                @pl.when(is_owner(layer))
                def _():
                    pltpu.make_async_copy(out4.at[layer], in4.at[head], came4.at[head]).start()

                @pl.when(jnp.logical_not(is_owner(layer)))
                def _():
                    to_owner(layer).start()

                square[0] += jnp.sum(mix_sum * mix_sum, axis=0, keepdims=True) + (
                    1.0 / lax.axis_size("dp")
                ) * jnp.sum(vec_sum * vec_sum, axis=0, keepdims=True)

    stages = (
        ("dp", dp, all_dp, dp_sent, dp_came),
        ("section", section, all_section, section_sent, section_came),
        ("tp", tp, all_tp, tp_sent, tp_came),
    )
    for index, (name, me, slots, sent, came) in enumerate(stages):
        count = lax.axis_size(name)

        def copy_to(peer, index=index, name=name, me=me, slots=slots, sent=sent, came=came):
            return remote(
                square.at[index], slots.at[me], sent.at[peer], came.at[me], **{name: peer}
            )

        def copy_from(peer, index=index, name=name, slots=slots, sent=sent, came=came):
            return remote(
                square.at[index], slots.at[peer], sent.at[peer], came.at[peer], **{name: peer}
            )

        slots[me] = square[index]

        @pl.loop(1, count)
        def _(step):
            copy_to(lax.rem(me + step, count)).start()

        @pl.loop(1, count)
        def _(step):
            copy_from(lax.rem(me + step, count)).wait_recv()

        square[index + 1] = jnp.sum(slots[...], axis=0)

        @pl.loop(1, count)
        def _(step):
            copy_to(lax.rem(me + step, count)).wait_send()

    total = jnp.sum(square[3], axis=-1, keepdims=True)
    scale_ref[...] = jnp.broadcast_to(lax.rsqrt(total / param_count + GRAD_EPS), scale_ref.shape)

    @pl.loop(0, heads)
    def _(item):
        remote(out4.at[0], in4.at[item], sent4.at[0], came4.at[item], tp=sibling).wait_recv()

    raw_ref[...] = in4[...]

    for other_pair in range(pairs):
        item, goes, mine, to_dp, to_tp = x_plan(other_pair)

        @pl.when(goes & jnp.logical_not(mine))
        def _():
            columns = pl.ds(pl.multiple_of(item * size, size), size)
            remote(
                x_ref.at[:, :, columns], x_in, x_sent.at[other_pair], x_came, tp=to_tp, dp=to_dp
            ).wait_send()

    @pl.loop(low, high_end)
    def _(to_unit):
        for bit in range(2):
            to_section = to_unit * 2 + bit
            for to_core in range(2):

                @pl.when(jnp.logical_not((to_section == section) & (core == to_core)))
                def _():
                    rows = pl.ds(to_core * half, half)
                    remote(
                        stage.at[0],
                        params.at[section],
                        p_sent.at[to_section, to_core],
                        p_came.at[section],
                        tp=sibling,
                    ).wait_send()
                    remote(
                        mix_ref.at[0, rows],
                        weights.at[section, rows],
                        w_sent.at[to_section, to_core],
                        w_came.at[section],
                        tp=sibling,
                    ).wait_send()

    @pl.when(active)
    def _():
        @pl.loop(0, layers)
        def _(layer):
            forward_half(layer).wait_send()
            exchange1(layer).wait_send()
            exchange2(layer).wait_send()
            exchange3(layer).wait_send()

            @pl.when(jnp.logical_not(is_owner(layer)))
            def _():
                to_owner(layer).wait_send()


def shards(inputs, norm_gain, norm_bias, mix):
    sections, tps, replicas = (lax.axis_size(name) for name in ("section", "tp", "dp"))
    batches, block, features = inputs.shape
    heads, size = mix.shape[1], mix.shape[2]
    rows = batches * block
    param_count = sections * tps * (2 * features + heads * size * size)
    loss_scale = 1.0 / math.sqrt(rows * replicas)
    piece = size // 8 + 8
    f32, bf16 = jnp.float32, jnp.bfloat16
    dma = pltpu.SemaphoreType.DMA
    flops = 3 * 2 * sections * rows * size * size
    raw, scale = pl.pallas_call(
        functools.partial(relay_kernel, loss_scale, float(param_count)),
        out_shape=(
            jax.ShapeDtypeStruct((heads, piece, size), f32),
            jax.ShapeDtypeStruct((1, size), f32),
        ),
        in_specs=[
            pl.BlockSpec(memory_space=pl.ANY),
            pl.BlockSpec(memory_space=pltpu.VMEM),
            pl.BlockSpec(memory_space=pltpu.VMEM),
            pl.BlockSpec(memory_space=pl.ANY),
        ],
        out_specs=[pl.BlockSpec(memory_space=pltpu.VMEM)] * 2,
        scratch_shapes=[
            pltpu.VMEM((batches, block, size), bf16),
            pltpu.VMEM((heads, 2, size), f32),
            pltpu.VMEM((sections, 2, size), f32),
            pltpu.VMEM((sections, size, size), bf16),
            pltpu.VMEM((rows, size), bf16),
            pltpu.VMEM((sections, rows, size), f32),
            pltpu.VMEM((sections, rows, size), f32),
            pltpu.VMEM((sections, rows, size), bf16),
            pltpu.VMEM((sections, rows, size), f32),
            pltpu.VMEM((sections, size, size), f32),
            pltpu.VMEM((sections, 8, size), f32),
            pltpu.VMEM((sections, size // 2 + 8, size), f32),
            pltpu.VMEM((sections, size // 4 + 8, size), f32),
            pltpu.VMEM((sections, piece, size), f32),
            pltpu.VMEM((sections, piece, size), f32),
            pltpu.VMEM((sections, size // 2 + 8, size), f32),
            pltpu.VMEM((sections, size // 4 + 8, size), f32),
            pltpu.VMEM((sections, piece, size), f32),
            pltpu.VMEM((heads, piece, size), f32),
            pltpu.VMEM((4, 1, size), f32),
            pltpu.VMEM((replicas, 1, size), f32),
            pltpu.VMEM((sections, 1, size), f32),
            pltpu.VMEM((tps, 1, size), f32),
            dma((replicas // 2,)),
            dma,
            dma((sections, 2)),
            dma((sections,)),
            dma((sections, 2)),
            dma((sections,)),
            dma((sections,)),
            dma((sections,)),
            dma((sections,)),
            dma((sections,)),
            dma((sections,)),
            dma((sections,)),
            dma((sections,)),
            dma((sections,)),
            dma((sections,)),
            dma((heads,)),
            dma((replicas,)),
            dma((replicas,)),
            dma((sections,)),
            dma((sections,)),
            dma((tps,)),
            dma((tps,)),
        ],
        compiler_params=pltpu.CompilerParams(
            vmem_limit_bytes=40 << 20, has_side_effects=True
        ),
        cost_estimate=pl.CostEstimate(
            flops=flops, bytes_accessed=4 << 20, transcendentals=sections * rows * size
        ),
        name="relay",
    )(inputs, norm_gain, norm_bias, mix[0])
    raw = raw * scale[None]
    return (
        raw[:, size // 8].reshape(1, features),
        raw[:, size // 8 + 1].reshape(1, features),
        raw[None, :, : size // 8],
    )


def solution(mesh):
    placed = (
        P(None, "dp", "tp"),
        P("section", "tp"),
        P("section", "tp"),
        P("section", "tp", None, None),
    )
    return jax.shard_map(
        shards,
        mesh=mesh,
        in_specs=placed,
        out_specs=(P("section", "tp"), P("section", "tp"), P("section", "tp", "dp", None)),
        check_vma=False,
    )
```

```python
import functools
import math

import jax
import jax.numpy as jnp
from jax import lax
from jax.experimental import pallas as pl
from jax.experimental.pallas import tpu as pltpu
from jax.sharding import PartitionSpec as P

EPSILON = 1e-05
GRAD_EPS = 1e-06
GELU_K = math.sqrt(2.0 / math.pi)
GELU_C = 0.044715


def forward_layer(wide, gain, bias, weights):
    mean = jnp.mean(wide, axis=-1, keepdims=True)
    centred = wide - mean
    inv_std = lax.rsqrt(jnp.mean(centred * centred, axis=-1, keepdims=True) + EPSILON)
    normed = centred * inv_std
    pre = normed * gain + bias
    square = pre * pre
    tangent = jnp.tanh(pre * (GELU_K + (GELU_K * GELU_C) * square))
    half = 0.5 + 0.5 * tangent
    act = pre * half
    slope = half + act * (1.0 - tangent) * (GELU_K + (3.0 * GELU_K * GELU_C) * square)
    act = act.astype(jnp.bfloat16)
    mixed = jnp.dot(act, weights, preferred_element_type=jnp.float32)
    return (wide + mixed).astype(jnp.bfloat16), normed, inv_std, act, slope


def backward_layer(grad, normed, inv_std, act, slope, gain, weights):
    grad_act = lax.dot_general(
        grad, weights, (((1,), (1,)), ((), ())), preferred_element_type=jnp.float32
    )
    mix_part = lax.dot_general(
        act, grad, (((0,), (0,)), ((), ())), preferred_element_type=jnp.float32
    )
    grad_pre = grad_act * slope
    gain_term = grad_pre * normed
    grad_norm = grad_pre * gain
    first = jnp.mean(grad_norm, axis=-1, keepdims=True)
    second = jnp.mean(gain_term * gain, axis=-1, keepdims=True)
    grad_in = grad.astype(jnp.float32) + inv_std * (grad_norm - first - normed * second)
    gain_part = jnp.sum(gain_term, axis=0, keepdims=True)
    bias_part = jnp.sum(grad_pre, axis=0, keepdims=True)
    return grad_in.astype(jnp.bfloat16), mix_part, gain_part, bias_part


MESH = pl.DeviceIdType.MESH
LAG_CORE = 3
LAG_CHIP = 8
AHEAD = 2


def relay_kernel(
    loss_scale,
    param_count,
    x_ref,
    gain_ref,
    bias_ref,
    mix_ref,
    raw_ref,
    scale_ref,
    x_in,
    rows_in,
    stage,
    params,
    weights,
    flow,
    normed_s,
    inv_s,
    act_s,
    slope_s,
    part_mix,
    part_vec,
    out1,
    out2,
    out4,
    in1,
    in2,
    in4,
    square,
    all_column,
    all_plane,
    rows_came,
    x_sent,
    x_came,
    w_sent,
    w_came,
    p_sent,
    p_came,
    f_sent,
    f_came,
    sent1,
    sent2,
    sent4,
    came1,
    came2,
    came4,
    column_sent,
    column_came,
    plane_sent,
    plane_came,
):
    section, tp, dp = (lax.axis_index(name) for name in ("section", "tp", "dp"))
    layers = weights.shape[0]
    heads = mix_ref.shape[0]
    size = mix_ref.shape[1]
    half, quarter, eighth = size // 2, size // 4, size // 8
    pairs = lax.axis_size("dp") // 2
    core, high = lax.rem(tp, 2), lax.div(tp, 2)
    unit, z_bit = lax.div(section, 2), lax.rem(section, 2)
    pair, y_bit = lax.div(dp, 2), lax.rem(dp, 2)
    place = unit * pairs + pair
    kin = lax.div(place, heads)
    head = place - kin * heads
    active = place < 2 * heads
    owner_tp = high * 2 + kin
    part = core * 4 + y_bit * 2 + z_bit

    def remote(source, target, sent, came, **where):
        return pltpu.make_async_remote_copy(
            src_ref=source,
            dst_ref=target,
            send_sem=sent,
            recv_sem=came,
            device_id=where,
            device_id_type=MESH,
        )

    def send(is_here, source, target, sent, came, **where):
        @pl.when(is_here)
        def _():
            pltpu.make_async_copy(source, target, came).start()

        @pl.when(jnp.logical_not(is_here))
        def _():
            remote(source, target, sent, came, **where).start()

    for index, ref in enumerate((gain_ref, bias_ref)):
        pltpu.make_async_copy(ref, rows_in.at[index], rows_came.at[index]).start()
    sections, dps = lax.axis_size("section"), lax.axis_size("dp")
    column, x_place = lax.rem(section, 4), lax.div(section, 4)
    barrier = pltpu.get_barrier_semaphore()

    def greet(**where):
        pl.semaphore_signal(barrier, inc=1, device_id=where, device_id_type=MESH)

    greeted = 0
    for x_step in range(1, sections // 4):
        for step in range(1, dps):
            greet(
                section=lax.rem(x_place + x_step, sections // 4) * 4 + column,
                dp=lax.rem(dp + step, dps),
            )
            greeted += 1
    for step in range(4):
        for to_core in range(2):
            greet(section=x_place * 4 + step, tp=(1 - high) * 2 + to_core)
            greeted += 1
    for step in range(1, sections):
        for to_core in range(2):
            greet(section=lax.rem(section + step, sections), tp=high * 2 + to_core)
            greeted += 1
    for step in range(1, dps):
        for to_core in range(2):
            greet(dp=lax.rem(dp + step, dps), tp=high * 2 + to_core)
            greeted += 1
    greet(section=unit * 2 + 1 - z_bit, dp=pair * 2 + 1 - y_bit)
    greet(tp=high * 2 + 1 - core)
    greeted += 2
    part_vec[...] = jnp.zeros_like(part_vec)
    square[...] = jnp.zeros_like(square)
    pl.semaphore_wait(barrier, greeted)

    def x_plan(other_pair):
        here = unit * pairs + other_pair
        goes = (lax.div(here, heads) == core) & (y_bit == z_bit)
        to_dp = other_pair * 2 + lax.rem(pair, 2)
        to_core = lax.div(dp, 4)
        mine = (to_dp == dp) & (to_core == core)
        return here - core * heads, goes, mine, to_dp, high * 2 + to_core

    for other_pair in range(pairs):
        item, goes, mine, to_dp, to_tp = x_plan(other_pair)

        @pl.when(goes)
        def _():
            columns = pl.ds(pl.multiple_of(item * size, size), size)
            send(
                mine,
                x_ref.at[:, :, columns],
                x_in,
                x_sent.at[other_pair],
                x_came,
                tp=to_tp,
                dp=to_dp,
            )

    for index, ref in enumerate((gain_ref, bias_ref)):
        pltpu.make_async_copy(ref, rows_in.at[index], rows_came.at[index]).wait()
        for item in range(heads):
            columns = slice(item * size, (item + 1) * size)
            stage[item, index : index + 1] = rows_in[index, 0:1, columns]
    middle = lax.div(heads + pairs - 1 - pair, pairs)
    stop = lax.div(2 * heads + pairs - 1 - pair, pairs)
    low = jnp.where(core == 0, 0, middle)
    high_end = jnp.where(core == 0, middle, stop)

    @pl.loop(low, high_end)
    def _(to_unit):
        item = to_unit * pairs + pair - core * heads
        for bit in range(2):
            to_section = to_unit * 2 + bit
            for to_core in range(2):
                mine = (to_section == section) & (core == to_core)
                rows = pl.ds(to_core * half, half)
                to_tp = high * 2 + to_core
                send(
                    mine,
                    stage.at[item],
                    params.at[section],
                    p_sent.at[to_section, to_core],
                    p_came.at[section],
                    section=to_section,
                    tp=to_tp,
                )
                send(
                    mine,
                    mix_ref.at[item, rows],
                    weights.at[section, rows],
                    w_sent.at[to_section, to_core],
                    w_came.at[section],
                    section=to_section,
                    tp=to_tp,
                )

    sibling = high * 2 + 1 - core
    own_rows = pl.ds(pl.multiple_of(core * half, half), half)
    other_rows = pl.ds(pl.multiple_of((1 - core) * half, half), half)

    def forward_half(layer):
        own = weights.at[layer, own_rows]
        return remote(own, own, f_sent.at[layer], f_came.at[layer], tp=sibling)

    def pass_on(layer):
        own = weights.at[layer, own_rows]
        remote(own, own, w_sent.at[0, 0], w_came.at[layer], tp=sibling).wait_recv()
        forward_half(layer).start()

    def exchange1(layer):
        return remote(
            out1.at[layer], in1.at[layer], sent1.at[layer], came1.at[layer], tp=sibling
        )

    chip = y_bit * 2 + z_bit

    def exchange2(layer, flip):
        to_y = lax.rem(y_bit + flip // 2, 2)
        to_z = lax.rem(z_bit + flip % 2, 2)
        return remote(
            out2.at[layer, to_y * 2 + to_z],
            in2.at[layer, chip],
            sent2.at[layer, flip - 1],
            came2.at[layer, flip - 1],
            section=unit * 2 + to_z,
            dp=pair * 2 + to_y,
        )

    def to_owner(layer):
        return remote(
            out4.at[layer],
            in4.at[head],
            sent4.at[layer],
            came4.at[head],
            section=layer,
            tp=owner_tp,
            dp=part,
        )

    def is_owner(layer):
        return (layer == section) & (owner_tp == tp) & (part == dp)

    def rows_of(ref, layer, start, count):
        return ref[layer, pl.ds(pl.multiple_of(start, 8), count)]

    @pl.when(active)
    def _():
        remote(x_in, x_in, x_sent.at[0], x_came, tp=sibling).wait_recv()
        flow[...] = x_in[...].reshape(flow.shape)
        for layer in range(AHEAD):
            pass_on(layer)

        @pl.loop(0, layers)
        def _(layer):
            @pl.when(layer + AHEAD < layers)
            def _():
                pass_on(layer + AHEAD)

            remote(
                stage.at[0], params.at[layer], p_sent.at[0, 0], p_came.at[layer], tp=sibling
            ).wait_recv()
            theirs = weights.at[layer, other_rows]
            remote(theirs, theirs, f_sent.at[layer], f_came.at[layer], tp=sibling).wait_recv()
            wide = flow[...].astype(jnp.float32)
            out, normed, inv_std, act, slope = forward_layer(
                wide, params[layer, 0:1], params[layer, 1:2], weights[layer]
            )
            flow[...] = out
            normed_s[layer] = normed
            inv_s[layer] = jnp.broadcast_to(inv_std, normed.shape)
            act_s[layer] = act
            slope_s[layer] = slope

        flow[...] = (flow[...].astype(jnp.float32) * loss_scale).astype(jnp.bfloat16)

        @pl.loop(0, layers + LAG_CORE + LAG_CHIP)
        def _(tick):
            @pl.when(tick < layers)
            def _():
                layer = layers - 1 - tick
                grad_in, mix_part, gain_part, bias_part = backward_layer(
                    flow[...],
                    normed_s[layer],
                    inv_s[layer],
                    act_s[layer],
                    slope_s[layer],
                    params[layer, 0:1],
                    weights[layer],
                )
                flow[...] = grad_in
                part_mix[layer] = mix_part
                part_vec[layer, 0:1] = gain_part
                part_vec[layer, 1:2] = bias_part
                out1[layer, 0:half] = rows_of(part_mix, layer, (1 - core) * half, half)
                out1[layer, half:] = part_vec[layer]
                exchange1(layer).start()

            step2 = tick - LAG_CORE

            @pl.when((step2 >= 0) & (step2 < layers))
            def _():
                layer = layers - 1 - step2
                exchange1(layer).wait_recv()
                mix_half = rows_of(part_mix, layer, core * half, half) + in1[layer, 0:half]
                vec_half = part_vec[layer] + in1[layer, half:]
                for index in range(4):
                    out2[layer, index, 0:eighth] = mix_half[index * eighth : (index + 1) * eighth]
                    out2[layer, index, eighth:] = vec_half
                for flip in (3, 2, 1):
                    exchange2(layer, flip).start()
                in2[layer, chip] = out2[layer, chip]

            step3 = tick - LAG_CORE - LAG_CHIP

            @pl.when((step3 >= 0) & (step3 < layers))
            def _():
                layer = layers - 1 - step3
                for flip in (1, 2, 3):
                    exchange2(layer, flip).wait_recv()
                whole = (in2[layer, 0] + in2[layer, 1]) + (in2[layer, 2] + in2[layer, 3])
                mix_sum, vec_sum = whole[:eighth], whole[eighth:]
                out4[layer] = whole

                @pl.when(is_owner(layer))
                def _():
                    pltpu.make_async_copy(out4.at[layer], in4.at[head], came4.at[head]).start()

                @pl.when(jnp.logical_not(is_owner(layer)))
                def _():
                    to_owner(layer).start()

                square[0] += jnp.sum(mix_sum * mix_sum, axis=0, keepdims=True) + (
                    1.0 / lax.axis_size("dp")
                ) * jnp.sum(vec_sum * vec_sum, axis=0, keepdims=True)

    def column_place(step):
        to_column = lax.rem(column + lax.div(step, 4), 4)
        to_tp = lax.rem(tp + lax.rem(step, 4), 4)
        return to_column * 4 + to_tp, dict(section=x_place * 4 + to_column, tp=to_tp)

    def plane_place(step):
        to_x = lax.rem(x_place + lax.div(step, dps), sections // 4)
        to_dp = lax.rem(dp + lax.rem(step, dps), dps)
        return to_x * dps + to_dp, dict(section=to_x * 4 + column, dp=to_dp)

    stages = (
        (column_place, all_column, column_sent, column_came),
        (plane_place, all_plane, plane_sent, plane_came),
    )
    for index, (place_of, slots, sent, came) in enumerate(stages):
        count = slots.shape[0]
        mine, _ = place_of(0)
        slots[mine] = square[index]

        def copy_to(step, index=index, place_of=place_of, slots=slots, sent=sent, came=came):
            place, where = place_of(step)
            here, _ = place_of(0)
            return remote(square.at[index], slots.at[here], sent.at[place], came.at[here], **where)

        def copy_from(step, index=index, place_of=place_of, slots=slots, sent=sent, came=came):
            place, where = place_of(step)
            return remote(square.at[index], slots.at[place], sent.at[place], came.at[place], **where)

        for step in range(1, count):
            copy_to(step).start()
        for step in range(1, count):
            copy_from(step).wait_recv()
        square[index + 1] = jnp.sum(slots[...], axis=0)

    total = jnp.sum(square[2], axis=-1, keepdims=True)
    scale_ref[...] = jnp.broadcast_to(lax.rsqrt(total / param_count + GRAD_EPS), scale_ref.shape)

    @pl.loop(0, heads)
    def _(item):
        remote(out4.at[0], in4.at[item], sent4.at[0], came4.at[item], tp=sibling).wait_recv()

    raw_ref[...] = in4[...]

    for index, (place_of, slots, sent, came) in enumerate(stages):

        @pl.loop(1, slots.shape[0])
        def _(step, index=index, place_of=place_of, slots=slots, sent=sent, came=came):
            place, where = place_of(step)
            remote(
                square.at[index], slots.at[place], sent.at[place], came.at[place], **where
            ).wait_send()

    for other_pair in range(pairs):
        item, goes, mine, to_dp, to_tp = x_plan(other_pair)

        @pl.when(goes & jnp.logical_not(mine))
        def _():
            columns = pl.ds(pl.multiple_of(item * size, size), size)
            remote(
                x_ref.at[:, :, columns], x_in, x_sent.at[other_pair], x_came, tp=to_tp, dp=to_dp
            ).wait_send()

    @pl.loop(low, high_end)
    def _(to_unit):
        for bit in range(2):
            to_section = to_unit * 2 + bit
            for to_core in range(2):

                @pl.when(jnp.logical_not((to_section == section) & (core == to_core)))
                def _():
                    rows = pl.ds(to_core * half, half)
                    remote(
                        stage.at[0],
                        params.at[section],
                        p_sent.at[to_section, to_core],
                        p_came.at[section],
                        tp=sibling,
                    ).wait_send()
                    remote(
                        mix_ref.at[0, rows],
                        weights.at[section, rows],
                        w_sent.at[to_section, to_core],
                        w_came.at[section],
                        tp=sibling,
                    ).wait_send()

    @pl.when(active)
    def _():
        @pl.loop(0, layers)
        def _(layer):
            forward_half(layer).wait_send()
            exchange1(layer).wait_send()
            for flip in (1, 2, 3):
                exchange2(layer, flip).wait_send()

            @pl.when(jnp.logical_not(is_owner(layer)))
            def _():
                to_owner(layer).wait_send()


def shards(inputs, norm_gain, norm_bias, mix):
    sections, tps, replicas = (lax.axis_size(name) for name in ("section", "tp", "dp"))
    batches, block, features = inputs.shape
    heads, size = mix.shape[1], mix.shape[2]
    rows = batches * block
    param_count = sections * tps * (2 * features + heads * size * size)
    loss_scale = 1.0 / math.sqrt(rows * replicas)
    piece = size // 8 + 8
    f32, bf16 = jnp.float32, jnp.bfloat16
    dma = pltpu.SemaphoreType.DMA
    flops = 3 * 2 * sections * rows * size * size
    raw, scale = pl.pallas_call(
        functools.partial(relay_kernel, loss_scale, float(param_count)),
        out_shape=(
            jax.ShapeDtypeStruct((heads, piece, size), f32),
            jax.ShapeDtypeStruct((1, size), f32),
        ),
        in_specs=[
            pl.BlockSpec(memory_space=pl.ANY),
            pl.BlockSpec(memory_space=pl.ANY),
            pl.BlockSpec(memory_space=pl.ANY),
            pl.BlockSpec(memory_space=pl.ANY),
        ],
        out_specs=[pl.BlockSpec(memory_space=pltpu.VMEM)] * 2,
        scratch_shapes=[
            pltpu.VMEM((batches, block, size), bf16),
            pltpu.VMEM((2, 1, features), f32),
            pltpu.VMEM((heads, 2, size), f32),
            pltpu.VMEM((sections, 2, size), f32),
            pltpu.VMEM((sections, size, size), bf16),
            pltpu.VMEM((rows, size), bf16),
            pltpu.VMEM((sections, rows, size), f32),
            pltpu.VMEM((sections, rows, size), f32),
            pltpu.VMEM((sections, rows, size), bf16),
            pltpu.VMEM((sections, rows, size), f32),
            pltpu.VMEM((sections, size, size), f32),
            pltpu.VMEM((sections, 8, size), f32),
            pltpu.VMEM((sections, size // 2 + 8, size), f32),
            pltpu.VMEM((sections, 4, piece, size), f32),
            pltpu.VMEM((sections, piece, size), f32),
            pltpu.VMEM((sections, size // 2 + 8, size), f32),
            pltpu.VMEM((sections, 4, piece, size), f32),
            pltpu.VMEM((heads, piece, size), f32),
            pltpu.VMEM((3, 1, size), f32),
            pltpu.VMEM((4 * tps, 1, size), f32),
            pltpu.VMEM((sections // 4 * replicas, 1, size), f32),
            dma((2,)),
            dma((replicas // 2,)),
            dma,
            dma((sections, 2)),
            dma((sections,)),
            dma((sections, 2)),
            dma((sections,)),
            dma((sections,)),
            dma((sections,)),
            dma((sections,)),
            dma((sections, 3)),
            dma((sections,)),
            dma((sections,)),
            dma((sections, 3)),
            dma((heads,)),
            dma((4 * tps,)),
            dma((4 * tps,)),
            dma((sections // 4 * replicas,)),
            dma((sections // 4 * replicas,)),
        ],
        compiler_params=pltpu.CompilerParams(
            vmem_limit_bytes=60 << 20, collective_id=0, has_side_effects=True
        ),
        cost_estimate=pl.CostEstimate(
            flops=flops, bytes_accessed=4 << 20, transcendentals=sections * rows * size
        ),
        name="relay",
    )(inputs, norm_gain, norm_bias, mix[0])
    raw = raw * scale[None]
    return (
        raw[:, size // 8].reshape(1, features),
        raw[:, size // 8 + 1].reshape(1, features),
        raw[None, :, : size // 8],
    )


def solution(mesh):
    placed = (
        P(None, "dp", "tp"),
        P("section", "tp"),
        P("section", "tp"),
        P("section", "tp", None, None),
    )
    return jax.shard_map(
        shards,
        mesh=mesh,
        in_specs=placed,
        out_specs=(P("section", "tp"), P("section", "tp"), P("section", "tp", "dp", None)),
        check_vma=False,
    )
```

```python
import functools
import math

import jax
import jax.numpy as jnp
from jax import lax
from jax.experimental import pallas as pl
from jax.experimental.pallas import tpu as pltpu
from jax.sharding import PartitionSpec as P

EPSILON = 1e-05
GRAD_EPS = 1e-06
GELU_K = math.sqrt(2.0 / math.pi)
GELU_C = 0.044715


def forward_layer(wide, gain, bias, weights):
    mean = jnp.mean(wide, axis=-1, keepdims=True)
    centred = wide - mean
    inv_std = lax.rsqrt(jnp.mean(centred * centred, axis=-1, keepdims=True) + EPSILON)
    normed = centred * inv_std
    pre = normed * gain + bias
    square = pre * pre
    tangent = jnp.tanh(pre * (GELU_K + (GELU_K * GELU_C) * square))
    half = 0.5 + 0.5 * tangent
    act = pre * half
    slope = half + act * (1.0 - tangent) * (GELU_K + (3.0 * GELU_K * GELU_C) * square)
    act = act.astype(jnp.bfloat16)
    mixed = jnp.dot(act, weights, preferred_element_type=jnp.float32)
    return (wide + mixed).astype(jnp.bfloat16), normed, inv_std, act, slope


def backward_layer(grad, normed, inv_std, act, slope, gain, weights):
    grad_act = lax.dot_general(
        grad, weights, (((1,), (1,)), ((), ())), preferred_element_type=jnp.float32
    )
    mix_part = lax.dot_general(
        act, grad, (((0,), (0,)), ((), ())), preferred_element_type=jnp.float32
    )
    grad_pre = grad_act * slope
    gain_term = grad_pre * normed
    grad_norm = grad_pre * gain
    first = jnp.mean(grad_norm, axis=-1, keepdims=True)
    second = jnp.mean(gain_term * gain, axis=-1, keepdims=True)
    grad_in = grad.astype(jnp.float32) + inv_std * (grad_norm - first - normed * second)
    gain_part = jnp.sum(gain_term, axis=0, keepdims=True)
    bias_part = jnp.sum(grad_pre, axis=0, keepdims=True)
    return grad_in.astype(jnp.bfloat16), mix_part, gain_part, bias_part


MESH = pl.DeviceIdType.MESH
LAG_CORE = 3
LAG_CHIP = 8
AHEAD = 5


def relay_kernel(
    loss_scale,
    param_count,
    x_ref,
    gain_ref,
    bias_ref,
    mix_ref,
    grads_ref,
    x_in,
    rows_in,
    stage,
    params,
    weights,
    flow,
    normed_s,
    inv_s,
    act_s,
    slope_s,
    part_mix,
    part_vec,
    out1,
    out2,
    out4,
    in1,
    in2,
    in4,
    square,
    all_column,
    all_plane,
    rows_came,
    x_sent,
    x_came,
    w_sent,
    w_came,
    p_sent,
    p_came,
    f_sent,
    f_came,
    sent1,
    sent2,
    sent4,
    came1,
    came2,
    came4,
    column_sent,
    column_came,
    plane_sent,
    plane_came,
):
    section, tp, dp = (lax.axis_index(name) for name in ("section", "tp", "dp"))
    layers = weights.shape[0]
    heads = mix_ref.shape[0]
    size = mix_ref.shape[1]
    half, eighth = size // 2, size // 8
    half_long, long = half + 2, eighth + 2
    pairs = lax.axis_size("dp") // 2
    core, high = lax.rem(tp, 2), lax.div(tp, 2)
    unit, z_bit = lax.div(section, 2), lax.rem(section, 2)
    pair, y_bit = lax.div(dp, 2), lax.rem(dp, 2)
    place = unit * pairs + pair
    kin = lax.div(place, heads)
    head = place - kin * heads
    active = place < 2 * heads
    owner_tp = high * 2 + kin
    part = core * 4 + y_bit * 2 + z_bit

    def remote(source, target, sent, came, **where):
        return pltpu.make_async_remote_copy(
            src_ref=source,
            dst_ref=target,
            send_sem=sent,
            recv_sem=came,
            device_id=where,
            device_id_type=MESH,
        )

    def send(is_here, source, target, sent, came, **where):
        @pl.when(is_here)
        def _():
            pltpu.make_async_copy(source, target, came).start()

        @pl.when(jnp.logical_not(is_here))
        def _():
            remote(source, target, sent, came, **where).start()

    for index, ref in enumerate((gain_ref, bias_ref)):
        pltpu.make_async_copy(ref, rows_in.at[index], rows_came.at[index]).start()
    sections, dps = lax.axis_size("section"), lax.axis_size("dp")
    column, x_place = lax.rem(section, 4), lax.div(section, 4)
    barrier = pltpu.get_barrier_semaphore()

    def greet(**where):
        pl.semaphore_signal(barrier, inc=1, device_id=where, device_id_type=MESH)

    greeted = 0
    for x_step in range(1, sections // 4):
        for step in range(1, dps):
            greet(
                section=lax.rem(x_place + x_step, sections // 4) * 4 + column,
                dp=lax.rem(dp + step, dps),
            )
            greeted += 1
    for step in range(4):
        for to_core in range(2):
            greet(section=x_place * 4 + step, tp=(1 - high) * 2 + to_core)
            greeted += 1
    for step in range(1, sections):
        for to_core in range(2):
            greet(section=lax.rem(section + step, sections), tp=high * 2 + to_core)
            greeted += 1
    for step in range(1, dps):
        for to_core in range(2):
            greet(dp=lax.rem(dp + step, dps), tp=high * 2 + to_core)
            greeted += 1
    greet(section=unit * 2 + 1 - z_bit, dp=pair * 2 + 1 - y_bit)
    greet(tp=high * 2 + 1 - core)
    greeted += 2
    square[...] = jnp.zeros_like(square)
    pl.semaphore_wait(barrier, greeted)

    def x_plan(other_pair):
        here = unit * pairs + other_pair
        goes = (lax.div(here, heads) == core) & (y_bit == z_bit)
        to_dp = other_pair * 2 + lax.rem(pair, 2)
        to_core = lax.div(dp, 4)
        mine = (to_dp == dp) & (to_core == core)
        return here - core * heads, goes, mine, to_dp, high * 2 + to_core

    for other_pair in range(pairs):
        item, goes, mine, to_dp, to_tp = x_plan(other_pair)

        @pl.when(goes)
        def _():
            columns = pl.ds(pl.multiple_of(item * size, size), size)
            send(
                mine,
                x_ref.at[:, :, columns],
                x_in,
                x_sent.at[other_pair],
                x_came,
                tp=to_tp,
                dp=to_dp,
            )

    for index, ref in enumerate((gain_ref, bias_ref)):
        pltpu.make_async_copy(ref, rows_in.at[index], rows_came.at[index]).wait()
        for item in range(heads):
            columns = slice(item * size, (item + 1) * size)
            stage[item, index : index + 1] = rows_in[index, 0:1, columns]
    middle = lax.div(heads + pairs - 1 - pair, pairs)
    stop = lax.div(2 * heads + pairs - 1 - pair, pairs)
    low = jnp.where(core == 0, 0, middle)
    high_end = jnp.where(core == 0, middle, stop)

    @pl.loop(low, high_end)
    def _(to_unit):
        item = to_unit * pairs + pair - core * heads
        for bit in range(2):
            to_section = to_unit * 2 + bit
            for to_core in range(2):
                mine = (to_section == section) & (core == to_core)
                rows = pl.ds(to_core * half, half)
                to_tp = high * 2 + to_core
                send(
                    mine,
                    stage.at[item],
                    params.at[section],
                    p_sent.at[to_section, to_core],
                    p_came.at[section],
                    section=to_section,
                    tp=to_tp,
                )
                send(
                    mine,
                    mix_ref.at[item, rows],
                    weights.at[section, rows],
                    w_sent.at[to_section, to_core],
                    w_came.at[section],
                    section=to_section,
                    tp=to_tp,
                )

    sibling = high * 2 + 1 - core
    own_rows = pl.ds(pl.multiple_of(core * half, half), half)
    other_rows = pl.ds(pl.multiple_of((1 - core) * half, half), half)

    def forward_half(layer):
        own = weights.at[layer, own_rows]
        return remote(own, own, f_sent.at[layer], f_came.at[layer], tp=sibling)

    def pass_on(layer):
        own = weights.at[layer, own_rows]
        remote(own, own, w_sent.at[0, 0], w_came.at[layer], tp=sibling).wait_recv()
        forward_half(layer).start()

    def exchange1(layer):
        return remote(
            out1.at[layer, 0:half_long], in1.at[layer, 0:half_long], sent1.at[layer], came1.at[layer], tp=sibling
        )

    chip = y_bit * 2 + z_bit

    def exchange2(layer, flip):
        to_y = lax.rem(y_bit + flip // 2, 2)
        to_z = lax.rem(z_bit + flip % 2, 2)
        return remote(
            out2.at[layer, to_y * 2 + to_z, 0:long],
            in2.at[layer, chip, 0:long],
            sent2.at[layer, flip - 1],
            came2.at[layer, flip - 1],
            section=unit * 2 + to_z,
            dp=pair * 2 + to_y,
        )

    def to_owner(layer):
        return remote(
            out4.at[layer, 0:long],
            in4.at[head, 0:long],
            sent4.at[layer],
            came4.at[head],
            section=layer,
            tp=owner_tp,
            dp=part,
        )

    def is_owner(layer):
        return (layer == section) & (owner_tp == tp) & (part == dp)

    def rows_of(ref, layer, start, count):
        return ref[layer, pl.ds(pl.multiple_of(start, 8), count)]

    @pl.when(active)
    def _():
        remote(x_in, x_in, x_sent.at[0], x_came, tp=sibling).wait_recv()
        flow[...] = x_in[...].reshape(flow.shape)
        for layer in range(AHEAD):
            pass_on(layer)

        @pl.loop(0, layers)
        def _(layer):
            @pl.when(layer + AHEAD < layers)
            def _():
                pass_on(layer + AHEAD)

            remote(
                stage.at[0], params.at[layer], p_sent.at[0, 0], p_came.at[layer], tp=sibling
            ).wait_recv()
            theirs = weights.at[layer, other_rows]
            remote(theirs, theirs, f_sent.at[layer], f_came.at[layer], tp=sibling).wait_recv()
            wide = flow[...].astype(jnp.float32)
            out, normed, inv_std, act, slope = forward_layer(
                wide, params[layer, 0:1], params[layer, 1:2], weights[layer]
            )
            flow[...] = out
            normed_s[layer] = normed
            inv_s[layer] = jnp.broadcast_to(inv_std, normed.shape)
            act_s[layer] = act
            slope_s[layer] = slope

        flow[...] = (flow[...].astype(jnp.float32) * loss_scale).astype(jnp.bfloat16)

        @pl.loop(0, layers + LAG_CORE + LAG_CHIP)
        def _(tick):
            @pl.when(tick < layers)
            def _():
                layer = layers - 1 - tick
                grad_in, mix_part, gain_part, bias_part = backward_layer(
                    flow[...],
                    normed_s[layer],
                    inv_s[layer],
                    act_s[layer],
                    slope_s[layer],
                    params[layer, 0:1],
                    weights[layer],
                )
                flow[...] = grad_in
                part_mix[layer] = mix_part
                part_vec[layer, 0:1] = gain_part
                part_vec[layer, 1:2] = bias_part
                out1[layer, 0:half] = rows_of(part_mix, layer, (1 - core) * half, half)
                out1[layer, half:half_long] = part_vec[layer]
                exchange1(layer).start()

            step2 = tick - LAG_CORE

            @pl.when((step2 >= 0) & (step2 < layers))
            def _():
                layer = layers - 1 - step2
                exchange1(layer).wait_recv()
                mix_half = rows_of(part_mix, layer, core * half, half) + in1[layer, 0:half]
                vec_half = part_vec[layer] + in1[layer, half:half_long]
                for index in range(4):
                    out2[layer, index, 0:eighth] = mix_half[index * eighth : (index + 1) * eighth]
                    out2[layer, index, eighth:long] = vec_half
                for flip in (3, 2, 1):
                    exchange2(layer, flip).start()
                in2[layer, chip, 0:long] = out2[layer, chip, 0:long]

            step3 = tick - LAG_CORE - LAG_CHIP

            @pl.when((step3 >= 0) & (step3 < layers))
            def _():
                layer = layers - 1 - step3
                for flip in (1, 2, 3):
                    exchange2(layer, flip).wait_recv()
                mix_sum, vec_sum = (
                    (in2[layer, 0, rows] + in2[layer, 1, rows])
                    + (in2[layer, 2, rows] + in2[layer, 3, rows])
                    for rows in (slice(0, eighth), slice(eighth, long))
                )
                out4[layer, 0:eighth] = mix_sum
                out4[layer, eighth:long] = vec_sum

                @pl.when(is_owner(layer))
                def _():
                    pltpu.make_async_copy(
                        out4.at[layer, 0:long], in4.at[head, 0:long], came4.at[head]
                    ).start()

                @pl.when(jnp.logical_not(is_owner(layer)))
                def _():
                    to_owner(layer).start()

                square[0] += jnp.sum(mix_sum * mix_sum, axis=0, keepdims=True) + (
                    1.0 / lax.axis_size("dp")
                ) * jnp.sum(vec_sum * vec_sum, axis=0, keepdims=True)

    def column_place(step):
        to_column = lax.rem(column + lax.div(step, 4), 4)
        to_tp = lax.rem(tp + lax.rem(step, 4), 4)
        return to_column * 4 + to_tp, dict(section=x_place * 4 + to_column, tp=to_tp)

    def plane_place(step):
        to_x = lax.rem(x_place + lax.div(step, dps), sections // 4)
        to_dp = lax.rem(dp + lax.rem(step, dps), dps)
        return to_x * dps + to_dp, dict(section=to_x * 4 + column, dp=to_dp)

    stages = (
        (column_place, all_column, column_sent, column_came),
        (plane_place, all_plane, plane_sent, plane_came),
    )
    for index, (place_of, slots, sent, came) in enumerate(stages):
        count = slots.shape[0]
        mine, _ = place_of(0)
        slots[mine] = square[index]

        def copy_to(step, index=index, place_of=place_of, slots=slots, sent=sent, came=came):
            place, where = place_of(step)
            here, _ = place_of(0)
            return remote(square.at[index], slots.at[here], sent.at[place], came.at[here], **where)

        def copy_from(step, index=index, place_of=place_of, slots=slots, sent=sent, came=came):
            place, where = place_of(step)
            return remote(square.at[index], slots.at[place], sent.at[place], came.at[place], **where)

        for step in range(1, count):
            copy_to(step).start()
        for step in range(1, count):
            copy_from(step).wait_recv()
        square[index + 1] = jnp.sum(slots[...], axis=0)

    total = jnp.sum(square[2], axis=-1, keepdims=True)
    scale = lax.rsqrt(total / param_count + GRAD_EPS)

    for item in range(heads):
        remote(
            out4.at[0, 0:long], in4.at[item, 0:long], sent4.at[0], came4.at[item], tp=sibling
        ).wait_recv()
        grads_ref[item, 0:long] = in4[item, 0:long] * scale

    for index, (place_of, slots, sent, came) in enumerate(stages):

        @pl.loop(1, slots.shape[0])
        def _(step, index=index, place_of=place_of, slots=slots, sent=sent, came=came):
            place, where = place_of(step)
            remote(
                square.at[index], slots.at[place], sent.at[place], came.at[place], **where
            ).wait_send()

    for other_pair in range(pairs):
        item, goes, mine, to_dp, to_tp = x_plan(other_pair)

        @pl.when(goes & jnp.logical_not(mine))
        def _():
            columns = pl.ds(pl.multiple_of(item * size, size), size)
            remote(
                x_ref.at[:, :, columns], x_in, x_sent.at[other_pair], x_came, tp=to_tp, dp=to_dp
            ).wait_send()

    @pl.loop(low, high_end)
    def _(to_unit):
        for bit in range(2):
            to_section = to_unit * 2 + bit
            for to_core in range(2):

                @pl.when(jnp.logical_not((to_section == section) & (core == to_core)))
                def _():
                    rows = pl.ds(to_core * half, half)
                    remote(
                        stage.at[0],
                        params.at[section],
                        p_sent.at[to_section, to_core],
                        p_came.at[section],
                        tp=sibling,
                    ).wait_send()
                    remote(
                        mix_ref.at[0, rows],
                        weights.at[section, rows],
                        w_sent.at[to_section, to_core],
                        w_came.at[section],
                        tp=sibling,
                    ).wait_send()

    @pl.when(active)
    def _():
        @pl.loop(0, layers)
        def _(layer):
            forward_half(layer).wait_send()
            exchange1(layer).wait_send()
            for flip in (1, 2, 3):
                exchange2(layer, flip).wait_send()

            @pl.when(jnp.logical_not(is_owner(layer)))
            def _():
                to_owner(layer).wait_send()


def shards(inputs, norm_gain, norm_bias, mix):
    sections, tps, replicas = (lax.axis_size(name) for name in ("section", "tp", "dp"))
    batches, block, features = inputs.shape
    heads, size = mix.shape[1], mix.shape[2]
    rows = batches * block
    param_count = sections * tps * (2 * features + heads * size * size)
    loss_scale = 1.0 / math.sqrt(rows * replicas)
    piece = size // 8 + 8
    f32, bf16 = jnp.float32, jnp.bfloat16
    dma = pltpu.SemaphoreType.DMA
    flops = 3 * 2 * sections * rows * size * size
    grads = pl.pallas_call(
        functools.partial(relay_kernel, loss_scale, float(param_count)),
        out_shape=jax.ShapeDtypeStruct((heads, piece, size), f32),
        in_specs=[
            pl.BlockSpec(memory_space=pl.ANY),
            pl.BlockSpec(memory_space=pl.ANY),
            pl.BlockSpec(memory_space=pl.ANY),
            pl.BlockSpec(memory_space=pl.ANY),
        ],
        out_specs=pl.BlockSpec(memory_space=pltpu.VMEM),
        scratch_shapes=[
            pltpu.VMEM((batches, block, size), bf16),
            pltpu.VMEM((2, 1, features), f32),
            pltpu.VMEM((heads, 2, size), f32),
            pltpu.VMEM((sections, 2, size), f32),
            pltpu.VMEM((sections, size, size), bf16),
            pltpu.VMEM((rows, size), bf16),
            pltpu.VMEM((sections, rows, size), f32),
            pltpu.VMEM((sections, rows, size), f32),
            pltpu.VMEM((sections, rows, size), bf16),
            pltpu.VMEM((sections, rows, size), f32),
            pltpu.VMEM((sections, size, size), f32),
            pltpu.VMEM((sections, 2, size), f32),
            pltpu.VMEM((sections, size // 2 + 8, size), f32),
            pltpu.VMEM((sections, 4, piece, size), f32),
            pltpu.VMEM((sections, piece, size), f32),
            pltpu.VMEM((sections, size // 2 + 8, size), f32),
            pltpu.VMEM((sections, 4, piece, size), f32),
            pltpu.VMEM((heads, piece, size), f32),
            pltpu.VMEM((3, 1, size), f32),
            pltpu.VMEM((4 * tps, 1, size), f32),
            pltpu.VMEM((sections // 4 * replicas, 1, size), f32),
            dma((2,)),
            dma((replicas // 2,)),
            dma,
            dma((sections, 2)),
            dma((sections,)),
            dma((sections, 2)),
            dma((sections,)),
            dma((sections,)),
            dma((sections,)),
            dma((sections,)),
            dma((sections, 3)),
            dma((sections,)),
            dma((sections,)),
            dma((sections, 3)),
            dma((heads,)),
            dma((4 * tps,)),
            dma((4 * tps,)),
            dma((sections // 4 * replicas,)),
            dma((sections // 4 * replicas,)),
        ],
        compiler_params=pltpu.CompilerParams(
            vmem_limit_bytes=60 << 20, collective_id=0, has_side_effects=True
        ),
        cost_estimate=pl.CostEstimate(
            flops=flops, bytes_accessed=4 << 20, transcendentals=sections * rows * size
        ),
        name="relay",
    )(inputs, norm_gain, norm_bias, mix[0])
    return (
        grads[:, size // 8].reshape(1, features),
        grads[:, size // 8 + 1].reshape(1, features),
        grads[None, :, : size // 8],
    )


def solution(mesh):
    placed = (
        P(None, "dp", "tp"),
        P("section", "tp"),
        P("section", "tp"),
        P("section", "tp", None, None),
    )
    return jax.shard_map(
        shards,
        mesh=mesh,
        in_specs=placed,
        out_specs=(P("section", "tp"), P("section", "tp"), P("section", "tp", "dp", None)),
        check_vma=False,
    )
```

```python
import functools
import math

import jax
import jax.numpy as jnp
from jax import lax
from jax.experimental import pallas as pl
from jax.experimental.pallas import tpu as pltpu
from jax.sharding import PartitionSpec as P

EPSILON = 1e-05
GRAD_EPS = 1e-06
GELU_K = math.sqrt(2.0 / math.pi)
GELU_C = 0.044715


def forward_layer(wide, gain, bias, weights):
    mean = jnp.mean(wide, axis=-1, keepdims=True)
    centred = wide - mean
    inv_std = lax.rsqrt(jnp.mean(centred * centred, axis=-1, keepdims=True) + EPSILON)
    normed = centred * inv_std
    pre = normed * gain + bias
    square = pre * pre
    tangent = jnp.tanh(pre * (GELU_K + (GELU_K * GELU_C) * square))
    half = 0.5 + 0.5 * tangent
    act = pre * half
    slope = half + act * (1.0 - tangent) * (GELU_K + (3.0 * GELU_K * GELU_C) * square)
    act = act.astype(jnp.bfloat16)
    mixed = jnp.dot(act, weights, preferred_element_type=jnp.float32)
    return (wide + mixed).astype(jnp.bfloat16), normed, inv_std, act, slope


def backward_layer(grad, normed, inv_std, act, slope, gain, weights, is_first):
    grad_act = lax.dot_general(
        grad, weights, (((1,), (1,)), ((), ())), preferred_element_type=jnp.float32
    )
    mix_part = lax.dot_general(
        act, grad, (((0,), (0,)), ((), ())), preferred_element_type=jnp.float32
    )
    grad_pre = grad_act * slope
    gain_term = grad_pre * normed
    gain_part = jnp.sum(gain_term, axis=0, keepdims=True)
    bias_part = jnp.sum(grad_pre, axis=0, keepdims=True)
    if is_first:
        return None, mix_part, gain_part, bias_part
    grad_norm = grad_pre * gain
    first = jnp.mean(grad_norm, axis=-1, keepdims=True)
    second = jnp.mean(gain_term * gain, axis=-1, keepdims=True)
    grad_in = grad.astype(jnp.float32) + inv_std * (grad_norm - first - normed * second)
    return grad_in.astype(jnp.bfloat16), mix_part, gain_part, bias_part


MESH = pl.DeviceIdType.MESH
LAG = 3
AHEAD = 4


def relay_kernel(
    loss_scale,
    param_count,
    x_ref,
    gain_ref,
    bias_ref,
    mix_ref,
    grads_ref,
    x_in,
    rows_in,
    stage,
    params,
    weights,
    flow,
    normed_s,
    inv_s,
    act_s,
    slope_s,
    part_mix,
    part_vec,
    out1,
    out2,
    out4,
    in1,
    in2,
    in4,
    square,
    all_column,
    all_plane,
    rows_came,
    x_sent,
    x_came,
    w_sent,
    w_came,
    p_sent,
    p_came,
    f_sent,
    f_came,
    sent1,
    sent2,
    sent4,
    came1,
    came2,
    came4,
    column_sent,
    column_came,
    plane_sent,
    plane_came,
):
    section, tp, dp = (lax.axis_index(name) for name in ("section", "tp", "dp"))
    layers = weights.shape[0]
    heads = mix_ref.shape[0]
    size = mix_ref.shape[1]
    half, eighth = size // 2, size // 8
    half_long, long = half + 2, eighth + 2
    pairs = lax.axis_size("dp") // 2
    core, high = lax.rem(tp, 2), lax.div(tp, 2)
    unit, z_bit = lax.div(section, 2), lax.rem(section, 2)
    pair, y_bit = lax.div(dp, 2), lax.rem(dp, 2)
    place = unit * pairs + pair
    kin = lax.div(place, heads)
    head = place - kin * heads
    active = place < 2 * heads
    owner_tp = high * 2 + kin
    part = core * 4 + y_bit * 2 + z_bit

    def remote(source, target, sent, came, **where):
        return pltpu.make_async_remote_copy(
            src_ref=source,
            dst_ref=target,
            send_sem=sent,
            recv_sem=came,
            device_id=where,
            device_id_type=MESH,
        )

    def send(is_here, source, target, sent, came, **where):
        @pl.when(is_here)
        def _():
            pltpu.make_async_copy(source, target, came).start()

        @pl.when(jnp.logical_not(is_here))
        def _():
            remote(source, target, sent, came, **where).start()

    for index, ref in enumerate((gain_ref, bias_ref)):
        pltpu.make_async_copy(ref, rows_in.at[index], rows_came.at[index]).start()
    sections, dps = lax.axis_size("section"), lax.axis_size("dp")
    column, x_place = lax.rem(section, 4), lax.div(section, 4)
    barrier = pltpu.get_barrier_semaphore()

    def greet(**where):
        pl.semaphore_signal(barrier, inc=1, device_id=where, device_id_type=MESH)

    greeted = 0
    for x_step in range(1, sections // 4):
        for step in range(1, dps):
            greet(
                section=lax.rem(x_place + x_step, sections // 4) * 4 + column,
                dp=lax.rem(dp + step, dps),
            )
            greeted += 1
    for step in range(4):
        for to_core in range(2):
            greet(section=x_place * 4 + step, tp=(1 - high) * 2 + to_core)
            greeted += 1
    for step in range(1, sections):
        for to_core in range(2):
            greet(section=lax.rem(section + step, sections), tp=high * 2 + to_core)
            greeted += 1
    for step in range(1, dps):
        for to_core in range(2):
            greet(dp=lax.rem(dp + step, dps), tp=high * 2 + to_core)
            greeted += 1
    greet(section=unit * 2 + 1 - z_bit, dp=pair * 2 + 1 - y_bit)
    greet(tp=high * 2 + 1 - core)
    greeted += 2
    square[...] = jnp.zeros_like(square)
    pl.semaphore_wait(barrier, greeted)

    def x_plan(other_pair):
        here = unit * pairs + other_pair
        goes = (lax.div(here, heads) == core) & (y_bit == z_bit)
        to_dp = other_pair * 2 + lax.rem(pair, 2)
        to_core = lax.div(dp, 4)
        mine = (to_dp == dp) & (to_core == core)
        return here - core * heads, goes, mine, to_dp, high * 2 + to_core

    for other_pair in range(pairs):
        item, goes, mine, to_dp, to_tp = x_plan(other_pair)

        @pl.when(goes)
        def _():
            columns = pl.ds(pl.multiple_of(item * size, size), size)
            send(
                mine,
                x_ref.at[:, :, columns],
                x_in,
                x_sent.at[other_pair],
                x_came,
                tp=to_tp,
                dp=to_dp,
            )

    for index, ref in enumerate((gain_ref, bias_ref)):
        pltpu.make_async_copy(ref, rows_in.at[index], rows_came.at[index]).wait()
        for item in range(heads):
            columns = slice(item * size, (item + 1) * size)
            stage[item, index : index + 1] = rows_in[index, 0:1, columns]
    middle = lax.div(heads + pairs - 1 - pair, pairs)
    stop = lax.div(2 * heads + pairs - 1 - pair, pairs)
    low = jnp.where(core == 0, 0, middle)
    high_end = jnp.where(core == 0, middle, stop)

    @pl.loop(0, high_end - low)
    def _(turn):
        to_unit = low + lax.rem(turn + unit, high_end - low)
        item = to_unit * pairs + pair - core * heads
        for bit in range(2):
            to_section = to_unit * 2 + bit
            for to_core in range(2):
                mine = (to_section == section) & (core == to_core)
                rows = pl.ds(to_core * half, half)
                to_tp = high * 2 + to_core
                send(
                    mine,
                    stage.at[item],
                    params.at[section],
                    p_sent.at[to_section, to_core],
                    p_came.at[section],
                    section=to_section,
                    tp=to_tp,
                )
                send(
                    mine,
                    mix_ref.at[item, rows],
                    weights.at[section, rows],
                    w_sent.at[to_section, to_core],
                    w_came.at[section],
                    section=to_section,
                    tp=to_tp,
                )

    sibling = high * 2 + 1 - core
    own_rows = pl.ds(pl.multiple_of(core * half, half), half)
    other_rows = pl.ds(pl.multiple_of((1 - core) * half, half), half)

    def forward_half(layer):
        own = weights.at[layer, own_rows]
        return remote(own, own, f_sent.at[layer], f_came.at[layer], tp=sibling)

    def pass_on(layer):
        own = weights.at[layer, own_rows]
        remote(own, own, w_sent.at[0, 0], w_came.at[layer], tp=sibling).wait_recv()
        forward_half(layer).start()

    def exchange1(layer):
        return remote(
            out1.at[layer, 0:half_long], in1.at[layer, 0:half_long], sent1.at[layer], came1.at[layer], tp=sibling
        )

    chip = y_bit * 2 + z_bit

    def exchange2(layer, flip):
        to_y = lax.rem(y_bit + flip // 2, 2)
        to_z = lax.rem(z_bit + flip % 2, 2)
        return remote(
            out2.at[layer, to_y * 2 + to_z, 0:long],
            in2.at[layer, chip, 0:long],
            sent2.at[layer, flip - 1],
            came2.at[layer, flip - 1],
            section=unit * 2 + to_z,
            dp=pair * 2 + to_y,
        )

    def to_owner(layer):
        return remote(
            out4.at[layer, 0:long],
            in4.at[head, 0:long],
            sent4.at[layer],
            came4.at[head],
            section=layer,
            tp=owner_tp,
            dp=part,
        )

    def is_owner(layer):
        return (layer == section) & (owner_tp == tp) & (part == dp)

    def start_to_owner(layer):
        @pl.when(is_owner(layer))
        def _():
            pltpu.make_async_copy(
                out4.at[layer, 0:long], in4.at[head, 0:long], came4.at[head]
            ).start()

        @pl.when(jnp.logical_not(is_owner(layer)))
        def _():
            to_owner(layer).start()

    def rows_of(ref, layer, start, count):
        return ref[layer, pl.ds(pl.multiple_of(start, 8), count)]

    @pl.when(active)
    def _():
        remote(x_in, x_in, x_sent.at[0], x_came, tp=sibling).wait_recv()
        flow[...] = x_in[...].reshape(flow.shape)
        for layer in range(AHEAD):
            pass_on(layer)

        @pl.loop(0, layers)
        def _(layer):
            @pl.when(layer + AHEAD < layers)
            def _():
                pass_on(layer + AHEAD)

            remote(
                stage.at[0], params.at[layer], p_sent.at[0, 0], p_came.at[layer], tp=sibling
            ).wait_recv()
            theirs = weights.at[layer, other_rows]
            remote(theirs, theirs, f_sent.at[layer], f_came.at[layer], tp=sibling).wait_recv()
            wide = flow[...].astype(jnp.float32)
            out, normed, inv_std, act, slope = forward_layer(
                wide, params[layer, 0:1], params[layer, 1:2], weights[layer]
            )
            flow[...] = out
            normed_s[layer] = normed
            inv_s[layer] = jnp.broadcast_to(inv_std, normed.shape)
            act_s[layer] = act
            slope_s[layer] = slope

        flow[...] = (flow[...].astype(jnp.float32) * loss_scale).astype(jnp.bfloat16)

        def back(layer, is_first=False):
            grad_in, mix_part, gain_part, bias_part = backward_layer(
                flow[...],
                normed_s[layer],
                inv_s[layer],
                act_s[layer],
                slope_s[layer],
                params[layer, 0:1],
                weights[layer],
                is_first,
            )
            if not is_first:
                flow[...] = grad_in
            part_mix[layer] = mix_part
            part_vec[layer, 0:1] = gain_part
            part_vec[layer, 1:2] = bias_part
            out1[layer, 0:half] = rows_of(part_mix, layer, (1 - core) * half, half)
            out1[layer, half:half_long] = part_vec[layer]

        def sum_cores(layer):
            mix_half = rows_of(part_mix, layer, core * half, half) + in1[layer, 0:half]
            vec_half = part_vec[layer] + in1[layer, half:half_long]
            for index in range(4):
                out2[layer, index, 0:eighth] = mix_half[index * eighth : (index + 1) * eighth]
                out2[layer, index, eighth:long] = vec_half

        def to_chips(layer):
            for flip in (3, 2, 1):
                exchange2(layer, flip).start()

        def sum_chips(group):
            for layer in group:
                for flip in (1, 2, 3):
                    exchange2(layer, flip).wait_recv()
            for layer in group:
                in2[layer, chip, 0:long] = out2[layer, chip, 0:long]
            squares, vec_squares = 0.0, 0.0
            for layer in group:
                mix_sum, vec_sum = (
                    (in2[layer, 0, rows] + in2[layer, 1, rows])
                    + (in2[layer, 2, rows] + in2[layer, 3, rows])
                    for rows in (slice(0, eighth), slice(eighth, long))
                )
                out4[layer, 0:eighth] = mix_sum
                out4[layer, eighth:long] = vec_sum
                squares += mix_sum * mix_sum
                vec_squares += vec_sum * vec_sum
            square[0] += jnp.sum(squares, axis=0, keepdims=True) + (
                1.0 / lax.axis_size("dp")
            ) * jnp.sum(vec_squares, axis=0, keepdims=True)

        @pl.loop(0, LAG)
        def _(tick):
            back(layers - 1 - tick)
            exchange1(layers - 1 - tick).start()

        @pl.loop(LAG, layers - 1)
        def _(tick):
            layer = layers - 1 - tick
            exchange1(layer + LAG).wait_recv()
            sum_cores(layer + LAG)
            back(layer)
            to_chips(layer + LAG)
            exchange1(layer).start()

        back(0, True)
        exchange1(0).start()
        for layer in range(LAG, 0, -1):
            exchange1(layer).wait_recv()
            sum_cores(layer)
            to_chips(layer)
        early = list(range(LAG + 3, layers))
        sum_chips(early[len(early) // 2 :])
        exchange1(0).wait_recv()
        sum_cores(0)
        to_chips(0)
        sum_chips(early[: len(early) // 2])
        sum_chips(list(range(LAG + 3)))

    def column_place(step):
        to_column = lax.rem(column + lax.div(step, 4), 4)
        to_tp = lax.rem(tp + lax.rem(step, 4), 4)
        return to_column * 4 + to_tp, dict(section=x_place * 4 + to_column, tp=to_tp)

    def plane_place(step):
        to_x = lax.rem(x_place + lax.div(step, dps), sections // 4)
        to_dp = lax.rem(dp + lax.rem(step, dps), dps)
        return to_x * dps + to_dp, dict(section=to_x * 4 + column, dp=to_dp)

    stages = (
        (column_place, all_column, column_sent, column_came),
        (plane_place, all_plane, plane_sent, plane_came),
    )
    for index, (place_of, slots, sent, came) in enumerate(stages):
        count = slots.shape[0]
        mine, _ = place_of(0)
        slots[mine] = square[index]

        def copy_to(step, index=index, place_of=place_of, slots=slots, sent=sent, came=came):
            place, where = place_of(step)
            here, _ = place_of(0)
            return remote(square.at[index], slots.at[here], sent.at[place], came.at[here], **where)

        def copy_from(step, index=index, place_of=place_of, slots=slots, sent=sent, came=came):
            place, where = place_of(step)
            return remote(square.at[index], slots.at[place], sent.at[place], came.at[place], **where)

        for step in range(1, count):
            copy_to(step).start()
        if index == 0:

            @pl.when(active)
            def _():
                @pl.loop(0, layers)
                def _(layer):
                    start_to_owner(lax.rem(layer + section, layers))

        for step in range(1, count):
            copy_from(step).wait_recv()
        square[index + 1] = jnp.sum(slots[...], axis=0)

    total = jnp.sum(square[2], axis=-1, keepdims=True)
    scale = lax.rsqrt(total / param_count + GRAD_EPS)

    for item in range(heads):
        remote(
            out4.at[0, 0:long], in4.at[item, 0:long], sent4.at[0], came4.at[item], tp=sibling
        ).wait_recv()
        grads_ref[item, 0:long] = in4[item, 0:long] * scale

    for index, (place_of, slots, sent, came) in enumerate(stages):

        @pl.loop(1, slots.shape[0])
        def _(step, index=index, place_of=place_of, slots=slots, sent=sent, came=came):
            place, where = place_of(step)
            remote(
                square.at[index], slots.at[place], sent.at[place], came.at[place], **where
            ).wait_send()

    for other_pair in range(pairs):
        item, goes, mine, to_dp, to_tp = x_plan(other_pair)

        @pl.when(goes & jnp.logical_not(mine))
        def _():
            columns = pl.ds(pl.multiple_of(item * size, size), size)
            remote(
                x_ref.at[:, :, columns], x_in, x_sent.at[other_pair], x_came, tp=to_tp, dp=to_dp
            ).wait_send()

    @pl.loop(low, high_end)
    def _(to_unit):
        for bit in range(2):
            to_section = to_unit * 2 + bit
            for to_core in range(2):

                @pl.when(jnp.logical_not((to_section == section) & (core == to_core)))
                def _():
                    rows = pl.ds(to_core * half, half)
                    remote(
                        stage.at[0],
                        params.at[section],
                        p_sent.at[to_section, to_core],
                        p_came.at[section],
                        tp=sibling,
                    ).wait_send()
                    remote(
                        mix_ref.at[0, rows],
                        weights.at[section, rows],
                        w_sent.at[to_section, to_core],
                        w_came.at[section],
                        tp=sibling,
                    ).wait_send()

    @pl.when(active)
    def _():
        @pl.loop(0, layers)
        def _(layer):
            forward_half(layer).wait_send()
            exchange1(layer).wait_send()
            for flip in (1, 2, 3):
                exchange2(layer, flip).wait_send()

            @pl.when(jnp.logical_not(is_owner(layer)))
            def _():
                to_owner(layer).wait_send()


def shards(inputs, norm_gain, norm_bias, mix):
    sections, tps, replicas = (lax.axis_size(name) for name in ("section", "tp", "dp"))
    batches, block, features = inputs.shape
    heads, size = mix.shape[1], mix.shape[2]
    rows = batches * block
    param_count = sections * tps * (2 * features + heads * size * size)
    loss_scale = 1.0 / math.sqrt(rows * replicas)
    piece = size // 8 + 8
    f32, bf16 = jnp.float32, jnp.bfloat16
    dma = pltpu.SemaphoreType.DMA
    flops = 3 * 2 * sections * rows * size * size
    grads = pl.pallas_call(
        functools.partial(relay_kernel, loss_scale, float(param_count)),
        out_shape=jax.ShapeDtypeStruct((heads, piece, size), f32),
        in_specs=[
            pl.BlockSpec(memory_space=pl.ANY),
            pl.BlockSpec(memory_space=pl.ANY),
            pl.BlockSpec(memory_space=pl.ANY),
            pl.BlockSpec(memory_space=pl.ANY),
        ],
        out_specs=pl.BlockSpec(memory_space=pltpu.VMEM),
        scratch_shapes=[
            pltpu.VMEM((batches, block, size), bf16),
            pltpu.VMEM((2, 1, features), f32),
            pltpu.VMEM((heads, 2, size), f32),
            pltpu.VMEM((sections, 2, size), f32),
            pltpu.VMEM((sections, size, size), bf16),
            pltpu.VMEM((rows, size), bf16),
            pltpu.VMEM((sections, rows, size), f32),
            pltpu.VMEM((sections, rows, size), f32),
            pltpu.VMEM((sections, rows, size), bf16),
            pltpu.VMEM((sections, rows, size), f32),
            pltpu.VMEM((sections, size, size), f32),
            pltpu.VMEM((sections, 2, size), f32),
            pltpu.VMEM((sections, size // 2 + 8, size), f32),
            pltpu.VMEM((sections, 4, piece, size), f32),
            pltpu.VMEM((sections, piece, size), f32),
            pltpu.VMEM((sections, size // 2 + 8, size), f32),
            pltpu.VMEM((sections, 4, piece, size), f32),
            pltpu.VMEM((heads, piece, size), f32),
            pltpu.VMEM((3, 1, size), f32),
            pltpu.VMEM((4 * tps, 1, size), f32),
            pltpu.VMEM((sections // 4 * replicas, 1, size), f32),
            dma((2,)),
            dma((replicas // 2,)),
            dma,
            dma((sections, 2)),
            dma((sections,)),
            dma((sections, 2)),
            dma((sections,)),
            dma((sections,)),
            dma((sections,)),
            dma((sections,)),
            dma((sections, 3)),
            dma((sections,)),
            dma((sections,)),
            dma((sections, 3)),
            dma((heads,)),
            dma((4 * tps,)),
            dma((4 * tps,)),
            dma((sections // 4 * replicas,)),
            dma((sections // 4 * replicas,)),
        ],
        compiler_params=pltpu.CompilerParams(
            vmem_limit_bytes=60 << 20, collective_id=0, has_side_effects=True
        ),
        cost_estimate=pl.CostEstimate(
            flops=flops, bytes_accessed=4 << 20, transcendentals=sections * rows * size
        ),
        name="relay",
    )(inputs, norm_gain, norm_bias, mix[0])
    return (
        grads[:, size // 8].reshape(1, features),
        grads[:, size // 8 + 1].reshape(1, features),
        grads[None, :, : size // 8],
    )


def solution(mesh):
    placed = (
        P(None, "dp", "tp"),
        P("section", "tp"),
        P("section", "tp"),
        P("section", "tp", None, None),
    )
    return jax.shard_map(
        shards,
        mesh=mesh,
        in_specs=placed,
        out_specs=(P("section", "tp"), P("section", "tp"), P("section", "tp", "dp", None)),
        check_vma=False,
    )
```

```python
import functools
import math

import jax
import jax.numpy as jnp
from jax import lax
from jax.experimental import pallas as pl
from jax.experimental.pallas import tpu as pltpu
from jax.sharding import PartitionSpec as P

EPSILON = 1e-05
GRAD_EPS = 1e-06
GELU_K = math.sqrt(2.0 / math.pi)
GELU_C = 0.044715


def forward_layer(wide, gain, bias, weights):
    mean = jnp.mean(wide, axis=-1, keepdims=True)
    centred = wide - mean
    inv_std = lax.rsqrt(jnp.mean(centred * centred, axis=-1, keepdims=True) + EPSILON)
    normed = centred * inv_std
    pre = normed * gain + bias
    square = pre * pre
    tangent = jnp.tanh(pre * (GELU_K + (GELU_K * GELU_C) * square))
    half = 0.5 + 0.5 * tangent
    act = pre * half
    slope = half + act * (1.0 - tangent) * (GELU_K + (3.0 * GELU_K * GELU_C) * square)
    act = act.astype(jnp.bfloat16)
    mixed = jnp.dot(act, weights, preferred_element_type=jnp.float32)
    return (wide + mixed).astype(jnp.bfloat16), normed, inv_std, act, slope


def backward_layer(grad, normed, inv_std, act, slope, gain, weights, is_first):
    grad_act = lax.dot_general(
        grad, weights, (((1,), (1,)), ((), ())), preferred_element_type=jnp.float32
    )
    mix_part = lax.dot_general(
        act, grad, (((0,), (0,)), ((), ())), preferred_element_type=jnp.float32
    )
    grad_pre = grad_act * slope
    gain_term = grad_pre * normed
    gain_part = jnp.sum(gain_term, axis=0, keepdims=True)
    bias_part = jnp.sum(grad_pre, axis=0, keepdims=True)
    if is_first:
        return None, mix_part, gain_part, bias_part
    grad_norm = grad_pre * gain
    first = jnp.mean(grad_norm, axis=-1, keepdims=True)
    second = jnp.mean(gain_term * gain, axis=-1, keepdims=True)
    grad_in = grad.astype(jnp.float32) + inv_std * (grad_norm - first - normed * second)
    return grad_in.astype(jnp.bfloat16), mix_part, gain_part, bias_part


MESH = pl.DeviceIdType.MESH
LAG = 2
AHEAD = 4


def relay_kernel(
    loss_scale,
    param_count,
    x_ref,
    gain_ref,
    bias_ref,
    mix_ref,
    grads_ref,
    x_in,
    rows_in,
    stage,
    params,
    weights,
    flow,
    normed_s,
    inv_s,
    act_s,
    slope_s,
    part_mix,
    part_vec,
    out1,
    out2,
    out4,
    in1,
    in2,
    in4,
    square,
    all_column,
    all_plane,
    rows_came,
    x_sent,
    x_came,
    w_sent,
    w_came,
    p_sent,
    p_came,
    f_sent,
    f_came,
    sent1,
    sent2,
    sent4,
    came1,
    came2,
    came4,
    column_sent,
    column_came,
    plane_sent,
    plane_came,
):
    section, tp, dp = (lax.axis_index(name) for name in ("section", "tp", "dp"))
    layers = weights.shape[0]
    heads = mix_ref.shape[0]
    size = mix_ref.shape[1]
    half, eighth = size // 2, size // 8
    half_long, long = half + 2, eighth + 2
    pairs = lax.axis_size("dp") // 2
    core, high = lax.rem(tp, 2), lax.div(tp, 2)
    unit, z_bit = lax.div(section, 2), lax.rem(section, 2)
    pair, y_bit = lax.div(dp, 2), lax.rem(dp, 2)
    place = unit * pairs + pair
    kin = lax.div(place, heads)
    head = place - kin * heads
    active = place < 2 * heads
    owner_tp = high * 2 + kin
    part = core * 4 + y_bit * 2 + z_bit

    def remote(source, target, sent, came, **where):
        return pltpu.make_async_remote_copy(
            src_ref=source,
            dst_ref=target,
            send_sem=sent,
            recv_sem=came,
            device_id=where,
            device_id_type=MESH,
        )

    def send(is_here, source, target, sent, came, **where):
        @pl.when(is_here)
        def _():
            pltpu.make_async_copy(source, target, came).start()

        @pl.when(jnp.logical_not(is_here))
        def _():
            remote(source, target, sent, came, **where).start()

    for index, ref in enumerate((gain_ref, bias_ref)):
        pltpu.make_async_copy(ref, rows_in.at[index], rows_came.at[index]).start()
    sections, dps = lax.axis_size("section"), lax.axis_size("dp")
    column, x_place = lax.rem(section, 4), lax.div(section, 4)
    barrier = pltpu.get_barrier_semaphore()

    def greet(**where):
        pl.semaphore_signal(barrier, inc=1, device_id=where, device_id_type=MESH)

    greeted = 0
    for x_step in range(1, sections // 4):
        for step in range(1, dps):
            greet(
                section=lax.rem(x_place + x_step, sections // 4) * 4 + column,
                dp=lax.rem(dp + step, dps),
            )
            greeted += 1
    for step in range(4):
        for to_core in range(2):
            greet(section=x_place * 4 + step, tp=(1 - high) * 2 + to_core)
            greeted += 1
    for step in range(1, sections):
        for to_core in range(2):
            greet(section=lax.rem(section + step, sections), tp=high * 2 + to_core)
            greeted += 1
    for step in range(1, dps):
        for to_core in range(2):
            greet(dp=lax.rem(dp + step, dps), tp=high * 2 + to_core)
            greeted += 1
    greet(section=unit * 2 + 1 - z_bit, dp=pair * 2 + 1 - y_bit)
    greet(tp=high * 2 + 1 - core)
    greeted += 2
    square[...] = jnp.zeros_like(square)
    pl.semaphore_wait(barrier, greeted)

    def x_plan(other_pair):
        here = unit * pairs + other_pair
        goes = (lax.div(here, heads) == core) & (y_bit == z_bit)
        to_dp = other_pair * 2 + lax.rem(pair, 2)
        to_core = lax.div(dp, 4)
        mine = (to_dp == dp) & (to_core == core)
        return here - core * heads, goes, mine, to_dp, high * 2 + to_core

    for other_pair in range(pairs):
        item, goes, mine, to_dp, to_tp = x_plan(other_pair)

        @pl.when(goes)
        def _():
            columns = pl.ds(pl.multiple_of(item * size, size), size)
            send(
                mine,
                x_ref.at[:, :, columns],
                x_in,
                x_sent.at[other_pair],
                x_came,
                tp=to_tp,
                dp=to_dp,
            )

    for index, ref in enumerate((gain_ref, bias_ref)):
        pltpu.make_async_copy(ref, rows_in.at[index], rows_came.at[index]).wait()
        for item in range(heads):
            columns = slice(item * size, (item + 1) * size)
            stage[item, index : index + 1] = rows_in[index, 0:1, columns]
    middle = lax.div(heads + pairs - 1 - pair, pairs)
    stop = lax.div(2 * heads + pairs - 1 - pair, pairs)
    low = jnp.where(core == 0, 0, middle)
    high_end = jnp.where(core == 0, middle, stop)

    @pl.loop(0, high_end - low)
    def _(turn):
        to_unit = low + lax.rem(turn + unit, high_end - low)
        item = to_unit * pairs + pair - core * heads
        for bit in range(2):
            to_section = to_unit * 2 + bit
            for to_core in range(2):
                mine = (to_section == section) & (core == to_core)
                rows = pl.ds(to_core * half, half)
                to_tp = high * 2 + to_core
                send(
                    mine,
                    stage.at[item],
                    params.at[section],
                    p_sent.at[to_section, to_core],
                    p_came.at[section],
                    section=to_section,
                    tp=to_tp,
                )
                send(
                    mine,
                    mix_ref.at[item, rows],
                    weights.at[section, rows],
                    w_sent.at[to_section, to_core],
                    w_came.at[section],
                    section=to_section,
                    tp=to_tp,
                )

    sibling = high * 2 + 1 - core
    own_rows = pl.ds(pl.multiple_of(core * half, half), half)
    other_rows = pl.ds(pl.multiple_of((1 - core) * half, half), half)

    def forward_half(layer):
        own = weights.at[layer, own_rows]
        return remote(own, own, f_sent.at[layer], f_came.at[layer], tp=sibling)

    def pass_on(layer):
        own = weights.at[layer, own_rows]
        remote(own, own, w_sent.at[0, 0], w_came.at[layer], tp=sibling).wait_recv()
        forward_half(layer).start()

    def both(couple):
        return pl.ds(2 * couple, 2)

    def exchange1(couple):
        return remote(
            out1.at[both(couple), 0:half_long],
            in1.at[both(couple), 0:half_long],
            sent1.at[couple],
            came1.at[couple],
            tp=sibling,
        )

    chip = y_bit * 2 + z_bit

    def exchange2(couple, flip):
        to_y = lax.rem(y_bit + flip // 2, 2)
        to_z = lax.rem(z_bit + flip % 2, 2)
        return remote(
            out2.at[to_y * 2 + to_z, both(couple), 0:long],
            in2.at[chip, both(couple), 0:long],
            sent2.at[couple, flip - 1],
            came2.at[couple, flip - 1],
            section=unit * 2 + to_z,
            dp=pair * 2 + to_y,
        )

    def to_owner(layer):
        return remote(
            out4.at[layer, 0:long],
            in4.at[head, 0:long],
            sent4.at[layer],
            came4.at[head],
            section=layer,
            tp=owner_tp,
            dp=part,
        )

    def is_owner(layer):
        return (layer == section) & (owner_tp == tp) & (part == dp)

    def start_to_owner(layer):
        @pl.when(is_owner(layer))
        def _():
            pltpu.make_async_copy(
                out4.at[layer, 0:long], in4.at[head, 0:long], came4.at[head]
            ).start()

        @pl.when(jnp.logical_not(is_owner(layer)))
        def _():
            to_owner(layer).start()

    def rows_of(ref, layer, start, count):
        return ref[layer, pl.ds(pl.multiple_of(start, 8), count)]

    @pl.when(active)
    def _():
        remote(x_in, x_in, x_sent.at[0], x_came, tp=sibling).wait_recv()
        flow[...] = x_in[...].reshape(flow.shape)
        for layer in range(AHEAD):
            pass_on(layer)

        @pl.loop(0, layers)
        def _(layer):
            @pl.when(layer + AHEAD < layers)
            def _():
                pass_on(layer + AHEAD)

            remote(
                stage.at[0], params.at[layer], p_sent.at[0, 0], p_came.at[layer], tp=sibling
            ).wait_recv()
            theirs = weights.at[layer, other_rows]
            remote(theirs, theirs, f_sent.at[layer], f_came.at[layer], tp=sibling).wait_recv()
            wide = flow[...].astype(jnp.float32)
            out, normed, inv_std, act, slope = forward_layer(
                wide, params[layer, 0:1], params[layer, 1:2], weights[layer]
            )
            flow[...] = out
            normed_s[layer] = normed
            inv_s[layer] = jnp.broadcast_to(inv_std, normed.shape)
            act_s[layer] = act
            slope_s[layer] = slope

        flow[...] = (flow[...].astype(jnp.float32) * loss_scale).astype(jnp.bfloat16)

        def back(layer, is_first=False):
            grad_in, mix_part, gain_part, bias_part = backward_layer(
                flow[...],
                normed_s[layer],
                inv_s[layer],
                act_s[layer],
                slope_s[layer],
                params[layer, 0:1],
                weights[layer],
                is_first,
            )
            if not is_first:
                flow[...] = grad_in
            part_mix[layer] = mix_part
            part_vec[layer, 0:1] = gain_part
            part_vec[layer, 1:2] = bias_part
            out1[layer, 0:half] = rows_of(part_mix, layer, (1 - core) * half, half)
            out1[layer, half:half_long] = part_vec[layer]

        def sum_cores(layer):
            mix_half = rows_of(part_mix, layer, core * half, half) + in1[layer, 0:half]
            vec_half = part_vec[layer] + in1[layer, half:half_long]
            for index in range(4):
                out2[index, layer, 0:eighth] = mix_half[index * eighth : (index + 1) * eighth]
                out2[index, layer, eighth:long] = vec_half

        def sum_pair(couple):
            exchange1(couple).wait_recv()
            sum_cores(2 * couple)
            sum_cores(2 * couple + 1)

        def to_chips(couple):
            for flip in (3, 2, 1):
                exchange2(couple, flip).start()

        def sum_chips(couples):
            for couple in couples:
                for flip in (1, 2, 3):
                    exchange2(couple, flip).wait_recv()
            group = [2 * couple + odd for couple in couples for odd in (0, 1)]
            for layer in group:
                in2[chip, layer, 0:long] = out2[chip, layer, 0:long]
            squares, vec_squares = 0.0, 0.0
            for layer in group:
                mix_sum, vec_sum = (
                    (in2[0, layer, rows] + in2[1, layer, rows])
                    + (in2[2, layer, rows] + in2[3, layer, rows])
                    for rows in (slice(0, eighth), slice(eighth, long))
                )
                out4[layer, 0:eighth] = mix_sum
                out4[layer, eighth:long] = vec_sum
                squares += mix_sum * mix_sum
                vec_squares += vec_sum * vec_sum
            square[0] += jnp.sum(squares, axis=0, keepdims=True) + (
                1.0 / lax.axis_size("dp")
            ) * jnp.sum(vec_squares, axis=0, keepdims=True)

        couples = layers // 2

        @pl.loop(0, LAG)
        def _(tick):
            couple = couples - 1 - tick
            back(2 * couple + 1)
            back(2 * couple)
            exchange1(couple).start()

        @pl.loop(LAG, couples - 1)
        def _(tick):
            couple = couples - 1 - tick
            sum_pair(couple + LAG)
            back(2 * couple + 1)
            to_chips(couple + LAG)
            back(2 * couple)
            exchange1(couple).start()

        back(1)
        back(0, True)
        exchange1(0).start()
        for couple in range(LAG, 0, -1):
            sum_pair(couple)
            to_chips(couple)
        sum_chips((6, 7))
        sum_pair(0)
        to_chips(0)
        sum_chips((4, 5))
        sum_chips((3, 2))
        sum_chips((1, 0))

    def column_place(step):
        to_column = lax.rem(column + lax.div(step, 4), 4)
        to_tp = lax.rem(tp + lax.rem(step, 4), 4)
        return to_column * 4 + to_tp, dict(section=x_place * 4 + to_column, tp=to_tp)

    def plane_place(step):
        to_x = lax.rem(x_place + lax.div(step, dps), sections // 4)
        to_dp = lax.rem(dp + lax.rem(step, dps), dps)
        return to_x * dps + to_dp, dict(section=to_x * 4 + column, dp=to_dp)

    stages = (
        (column_place, all_column, column_sent, column_came),
        (plane_place, all_plane, plane_sent, plane_came),
    )
    for index, (place_of, slots, sent, came) in enumerate(stages):
        count = slots.shape[0]
        mine, _ = place_of(0)
        slots[mine] = square[index]

        def copy_to(step, index=index, place_of=place_of, slots=slots, sent=sent, came=came):
            place, where = place_of(step)
            here, _ = place_of(0)
            return remote(square.at[index], slots.at[here], sent.at[place], came.at[here], **where)

        def copy_from(step, index=index, place_of=place_of, slots=slots, sent=sent, came=came):
            place, where = place_of(step)
            return remote(square.at[index], slots.at[place], sent.at[place], came.at[place], **where)

        for step in range(1, count):
            copy_to(step).start()
        if index == 0:

            @pl.when(active)
            def _():
                @pl.loop(0, layers)
                def _(layer):
                    start_to_owner(lax.rem(layer + section, layers))

        for step in range(1, count):
            copy_from(step).wait_recv()
        square[index + 1] = jnp.sum(slots[...], axis=0)

    total = jnp.sum(square[2], axis=-1, keepdims=True)
    scale = lax.rsqrt(total / param_count + GRAD_EPS)

    for item in range(heads):
        remote(
            out4.at[0, 0:long], in4.at[item, 0:long], sent4.at[0], came4.at[item], tp=sibling
        ).wait_recv()
        grads_ref[item, 0:long] = in4[item, 0:long] * scale

    for index, (place_of, slots, sent, came) in enumerate(stages):

        @pl.loop(1, slots.shape[0])
        def _(step, index=index, place_of=place_of, slots=slots, sent=sent, came=came):
            place, where = place_of(step)
            remote(
                square.at[index], slots.at[place], sent.at[place], came.at[place], **where
            ).wait_send()

    for other_pair in range(pairs):
        item, goes, mine, to_dp, to_tp = x_plan(other_pair)

        @pl.when(goes & jnp.logical_not(mine))
        def _():
            columns = pl.ds(pl.multiple_of(item * size, size), size)
            remote(
                x_ref.at[:, :, columns], x_in, x_sent.at[other_pair], x_came, tp=to_tp, dp=to_dp
            ).wait_send()

    @pl.loop(low, high_end)
    def _(to_unit):
        for bit in range(2):
            to_section = to_unit * 2 + bit
            for to_core in range(2):

                @pl.when(jnp.logical_not((to_section == section) & (core == to_core)))
                def _():
                    rows = pl.ds(to_core * half, half)
                    remote(
                        stage.at[0],
                        params.at[section],
                        p_sent.at[to_section, to_core],
                        p_came.at[section],
                        tp=sibling,
                    ).wait_send()
                    remote(
                        mix_ref.at[0, rows],
                        weights.at[section, rows],
                        w_sent.at[to_section, to_core],
                        w_came.at[section],
                        tp=sibling,
                    ).wait_send()

    @pl.when(active)
    def _():
        @pl.loop(0, layers)
        def _(layer):
            forward_half(layer).wait_send()

            @pl.when(jnp.logical_not(is_owner(layer)))
            def _():
                to_owner(layer).wait_send()

        @pl.loop(0, layers // 2)
        def _(couple):
            exchange1(couple).wait_send()
            for flip in (1, 2, 3):
                exchange2(couple, flip).wait_send()


def shards(inputs, norm_gain, norm_bias, mix):
    sections, tps, replicas = (lax.axis_size(name) for name in ("section", "tp", "dp"))
    batches, block, features = inputs.shape
    heads, size = mix.shape[1], mix.shape[2]
    rows = batches * block
    param_count = sections * tps * (2 * features + heads * size * size)
    loss_scale = 1.0 / math.sqrt(rows * replicas)
    piece = size // 8 + 8
    f32, bf16 = jnp.float32, jnp.bfloat16
    dma = pltpu.SemaphoreType.DMA
    flops = 3 * 2 * sections * rows * size * size
    grads = pl.pallas_call(
        functools.partial(relay_kernel, loss_scale, float(param_count)),
        out_shape=jax.ShapeDtypeStruct((heads, piece, size), f32),
        in_specs=[
            pl.BlockSpec(memory_space=pl.ANY),
            pl.BlockSpec(memory_space=pl.ANY),
            pl.BlockSpec(memory_space=pl.ANY),
            pl.BlockSpec(memory_space=pl.ANY),
        ],
        out_specs=pl.BlockSpec(memory_space=pltpu.VMEM),
        scratch_shapes=[
            pltpu.VMEM((batches, block, size), bf16),
            pltpu.VMEM((2, 1, features), f32),
            pltpu.VMEM((heads, 2, size), f32),
            pltpu.VMEM((sections, 2, size), f32),
            pltpu.VMEM((sections, size, size), bf16),
            pltpu.VMEM((rows, size), bf16),
            pltpu.VMEM((sections, rows, size), f32),
            pltpu.VMEM((sections, rows, size), f32),
            pltpu.VMEM((sections, rows, size), bf16),
            pltpu.VMEM((sections, rows, size), f32),
            pltpu.VMEM((sections, size, size), f32),
            pltpu.VMEM((sections, 2, size), f32),
            pltpu.VMEM((sections, size // 2 + 8, size), f32),
            pltpu.VMEM((4, sections, piece, size), f32),
            pltpu.VMEM((sections, piece, size), f32),
            pltpu.VMEM((sections, size // 2 + 8, size), f32),
            pltpu.VMEM((4, sections, piece, size), f32),
            pltpu.VMEM((heads, piece, size), f32),
            pltpu.VMEM((3, 1, size), f32),
            pltpu.VMEM((4 * tps, 1, size), f32),
            pltpu.VMEM((sections // 4 * replicas, 1, size), f32),
            dma((2,)),
            dma((replicas // 2,)),
            dma,
            dma((sections, 2)),
            dma((sections,)),
            dma((sections, 2)),
            dma((sections,)),
            dma((sections,)),
            dma((sections,)),
            dma((sections,)),
            dma((sections // 2, 3)),
            dma((sections,)),
            dma((sections,)),
            dma((sections // 2, 3)),
            dma((heads,)),
            dma((4 * tps,)),
            dma((4 * tps,)),
            dma((sections // 4 * replicas,)),
            dma((sections // 4 * replicas,)),
        ],
        compiler_params=pltpu.CompilerParams(
            vmem_limit_bytes=60 << 20, collective_id=0, has_side_effects=True
        ),
        cost_estimate=pl.CostEstimate(
            flops=flops, bytes_accessed=4 << 20, transcendentals=sections * rows * size
        ),
        name="relay",
    )(inputs, norm_gain, norm_bias, mix[0])
    return (
        grads[:, size // 8].reshape(1, features),
        grads[:, size // 8 + 1].reshape(1, features),
        grads[None, :, : size // 8],
    )


def solution(mesh):
    placed = (
        P(None, "dp", "tp"),
        P("section", "tp"),
        P("section", "tp"),
        P("section", "tp", None, None),
    )
    return jax.shard_map(
        shards,
        mesh=mesh,
        in_specs=placed,
        out_specs=(P("section", "tp"), P("section", "tp"), P("section", "tp", "dp", None)),
        check_vma=False,
    )
```

```python
import functools
import math

import jax
import jax.numpy as jnp
from jax import lax
from jax.experimental import pallas as pl
from jax.experimental.pallas import tpu as pltpu
from jax.sharding import PartitionSpec as P

EPSILON = 1e-05
GRAD_EPS = 1e-06
GELU_K = math.sqrt(2.0 / math.pi)
GELU_C = 0.044715


def forward_layer(wide, gain, bias, weights):
    mean = jnp.mean(wide, axis=-1, keepdims=True)
    centred = wide - mean
    inv_std = lax.rsqrt(jnp.mean(centred * centred, axis=-1, keepdims=True) + EPSILON)
    normed = centred * inv_std
    pre = normed * gain + bias
    square = pre * pre
    tangent = jnp.tanh(pre * (GELU_K + (GELU_K * GELU_C) * square))
    half = 0.5 + 0.5 * tangent
    act = pre * half
    slope = half + act * (1.0 - tangent) * (GELU_K + (3.0 * GELU_K * GELU_C) * square)
    act = act.astype(jnp.bfloat16)
    mixed = jnp.dot(act, weights, preferred_element_type=jnp.float32)
    return (wide + mixed).astype(jnp.bfloat16), normed, inv_std, act, slope


def backward_layer(grad, normed, inv_std, act, slope, gain, weights, is_first):
    grad_act = lax.dot_general(
        grad, weights, (((1,), (1,)), ((), ())), preferred_element_type=jnp.float32
    )
    mix_part = lax.dot_general(
        act, grad, (((0,), (0,)), ((), ())), preferred_element_type=jnp.float32
    )
    grad_pre = grad_act * slope
    gain_term = grad_pre * normed
    gain_part = jnp.sum(gain_term, axis=0, keepdims=True)
    bias_part = jnp.sum(grad_pre, axis=0, keepdims=True)
    if is_first:
        return None, mix_part, gain_part, bias_part
    grad_norm = grad_pre * gain
    first = jnp.mean(grad_norm, axis=-1, keepdims=True)
    second = jnp.mean(gain_term * gain, axis=-1, keepdims=True)
    grad_in = grad.astype(jnp.float32) + inv_std * (grad_norm - first - normed * second)
    return grad_in.astype(jnp.bfloat16), mix_part, gain_part, bias_part


MESH = pl.DeviceIdType.MESH
LAG = 2
AHEAD = 4


def relay_kernel(
    loss_scale,
    param_count,
    x_ref,
    gain_ref,
    bias_ref,
    mix_ref,
    grads_ref,
    x_in,
    rows_in,
    stage,
    params,
    weights,
    flow,
    normed_s,
    inv_s,
    act_s,
    slope_s,
    part_mix,
    part_vec,
    out1,
    out2,
    out4,
    in1,
    in2,
    in4,
    square,
    all_column,
    all_plane,
    rows_came,
    x_sent,
    x_came,
    w_sent,
    w_came,
    p_sent,
    p_came,
    f_sent,
    f_came,
    sent1,
    sent2,
    sent4,
    came1,
    came2,
    came4,
    column_sent,
    column_came,
    plane_sent,
    plane_came,
):
    section, tp, dp = (lax.axis_index(name) for name in ("section", "tp", "dp"))
    layers = weights.shape[0]
    heads = mix_ref.shape[0]
    size = mix_ref.shape[1]
    half, eighth = size // 2, size // 8
    half_long, long = half + 2, eighth + 2
    pairs = lax.axis_size("dp") // 2
    core, high = lax.rem(tp, 2), lax.div(tp, 2)
    unit, z_bit = lax.div(section, 2), lax.rem(section, 2)
    pair, y_bit = lax.div(dp, 2), lax.rem(dp, 2)
    place = unit * pairs + pair
    kin = lax.div(place, heads)
    head = place - kin * heads
    active = place < 2 * heads
    owner_tp = high * 2 + kin
    part = core * 4 + y_bit * 2 + z_bit

    def remote(source, target, sent, came, **where):
        return pltpu.make_async_remote_copy(
            src_ref=source,
            dst_ref=target,
            send_sem=sent,
            recv_sem=came,
            device_id=where,
            device_id_type=MESH,
        )

    def send(is_here, source, target, sent, came, **where):
        @pl.when(is_here)
        def _():
            pltpu.make_async_copy(source, target, came).start()

        @pl.when(jnp.logical_not(is_here))
        def _():
            remote(source, target, sent, came, **where).start()

    for index, ref in enumerate((gain_ref, bias_ref)):
        pltpu.make_async_copy(ref, rows_in.at[index], rows_came.at[index]).start()
    sections, dps = lax.axis_size("section"), lax.axis_size("dp")
    column, x_place = lax.rem(section, 4), lax.div(section, 4)
    barrier = pltpu.get_barrier_semaphore()

    def greet(**where):
        pl.semaphore_signal(barrier, inc=1, device_id=where, device_id_type=MESH)

    greeted = 0
    for x_step in range(1, sections // 4):
        for step in range(1, dps):
            greet(
                section=lax.rem(x_place + x_step, sections // 4) * 4 + column,
                dp=lax.rem(dp + step, dps),
            )
            greeted += 1
    for step in range(4):
        for to_core in range(2):
            greet(section=x_place * 4 + step, tp=(1 - high) * 2 + to_core)
            greeted += 1
    for step in range(1, sections):
        for to_core in range(2):
            greet(section=lax.rem(section + step, sections), tp=high * 2 + to_core)
            greeted += 1
    for step in range(1, dps):
        for to_core in range(2):
            greet(dp=lax.rem(dp + step, dps), tp=high * 2 + to_core)
            greeted += 1
    greet(section=unit * 2 + 1 - z_bit, dp=pair * 2 + 1 - y_bit)
    greet(tp=high * 2 + 1 - core)
    greeted += 2
    square[...] = jnp.zeros_like(square)
    pl.semaphore_wait(barrier, greeted)

    def x_plan(other_pair):
        here = unit * pairs + other_pair
        goes = (lax.div(here, heads) == core) & (y_bit == z_bit)
        to_dp = other_pair * 2 + lax.rem(pair, 2)
        to_core = lax.div(dp, 4)
        mine = (to_dp == dp) & (to_core == core)
        return here - core * heads, goes, mine, to_dp, high * 2 + to_core

    for other_pair in range(pairs):
        item, goes, mine, to_dp, to_tp = x_plan(other_pair)

        @pl.when(goes)
        def _():
            columns = pl.ds(pl.multiple_of(item * size, size), size)
            send(
                mine,
                x_ref.at[:, :, columns],
                x_in,
                x_sent.at[other_pair],
                x_came,
                tp=to_tp,
                dp=to_dp,
            )

    for index, ref in enumerate((gain_ref, bias_ref)):
        pltpu.make_async_copy(ref, rows_in.at[index], rows_came.at[index]).wait()
        for item in range(heads):
            columns = slice(item * size, (item + 1) * size)
            stage[item, index : index + 1] = rows_in[index, 0:1, columns]
    middle = lax.div(heads + pairs - 1 - pair, pairs)
    stop = lax.div(2 * heads + pairs - 1 - pair, pairs)
    low = jnp.where(core == 0, 0, middle)
    high_end = jnp.where(core == 0, middle, stop)

    @pl.loop(0, high_end - low)
    def _(turn):
        to_unit = low + lax.rem(turn + unit, high_end - low)
        item = to_unit * pairs + pair - core * heads
        for bit in range(2):
            to_section = to_unit * 2 + bit
            for to_core in range(2):
                mine = (to_section == section) & (core == to_core)
                rows = pl.ds(to_core * half, half)
                to_tp = high * 2 + to_core
                send(
                    mine,
                    stage.at[item],
                    params.at[section],
                    p_sent.at[to_section, to_core],
                    p_came.at[section],
                    section=to_section,
                    tp=to_tp,
                )
                send(
                    mine,
                    mix_ref.at[item, rows],
                    weights.at[section, rows],
                    w_sent.at[to_section, to_core],
                    w_came.at[section],
                    section=to_section,
                    tp=to_tp,
                )

    sibling = high * 2 + 1 - core
    own_rows = pl.ds(pl.multiple_of(core * half, half), half)
    other_rows = pl.ds(pl.multiple_of((1 - core) * half, half), half)

    def forward_half(layer):
        own = weights.at[layer, own_rows]
        return remote(own, own, f_sent.at[layer], f_came.at[layer], tp=sibling)

    def pass_on(layer):
        own = weights.at[layer, own_rows]
        remote(own, own, w_sent.at[0, 0], w_came.at[layer], tp=sibling).wait_recv()
        forward_half(layer).start()

    def both(couple):
        return pl.ds(2 * couple, 2)

    def exchange1(couple):
        return remote(
            out1.at[both(couple), 0:half_long],
            in1.at[both(couple), 0:half_long],
            sent1.at[couple],
            came1.at[couple],
            tp=sibling,
        )

    chip = y_bit * 2 + z_bit

    def exchange2(couple, flip):
        to_y = lax.rem(y_bit + flip // 2, 2)
        to_z = lax.rem(z_bit + flip % 2, 2)
        return remote(
            out2.at[to_y * 2 + to_z, both(couple), 0:long],
            in2.at[chip, both(couple), 0:long],
            sent2.at[couple, flip - 1],
            came2.at[couple, flip - 1],
            section=unit * 2 + to_z,
            dp=pair * 2 + to_y,
        )

    def to_owner(layer):
        return remote(
            out4.at[layer, 0:long],
            in4.at[head, 0:long],
            sent4.at[layer],
            came4.at[head],
            section=layer,
            tp=owner_tp,
            dp=part,
        )

    def is_owner(layer):
        return (layer == section) & (owner_tp == tp) & (part == dp)

    def start_to_owner(layer):
        @pl.when(is_owner(layer))
        def _():
            pltpu.make_async_copy(
                out4.at[layer, 0:long], in4.at[head, 0:long], came4.at[head]
            ).start()

        @pl.when(jnp.logical_not(is_owner(layer)))
        def _():
            to_owner(layer).start()

    def rows_of(ref, layer, start, count):
        return ref[layer, pl.ds(pl.multiple_of(start, 8), count)]

    @pl.when(active)
    def _():
        remote(x_in, x_in, x_sent.at[0], x_came, tp=sibling).wait_recv()
        flow[...] = x_in[...].reshape(flow.shape)
        for layer in range(AHEAD):
            pass_on(layer)

        @pl.loop(0, layers)
        def _(layer):
            @pl.when(layer + AHEAD < layers)
            def _():
                pass_on(layer + AHEAD)

            remote(
                stage.at[0], params.at[layer], p_sent.at[0, 0], p_came.at[layer], tp=sibling
            ).wait_recv()
            theirs = weights.at[layer, other_rows]
            remote(theirs, theirs, f_sent.at[layer], f_came.at[layer], tp=sibling).wait_recv()
            wide = flow[...].astype(jnp.float32)
            out, normed, inv_std, act, slope = forward_layer(
                wide, params[layer, 0:1], params[layer, 1:2], weights[layer]
            )
            flow[...] = out
            normed_s[layer] = normed
            inv_s[layer] = jnp.broadcast_to(inv_std, normed.shape)
            act_s[layer] = act
            slope_s[layer] = slope

        flow[...] = (flow[...].astype(jnp.float32) * loss_scale).astype(jnp.bfloat16)

        def back(layer, is_first=False):
            grad_in, mix_part, gain_part, bias_part = backward_layer(
                flow[...],
                normed_s[layer],
                inv_s[layer],
                act_s[layer],
                slope_s[layer],
                params[layer, 0:1],
                weights[layer],
                is_first,
            )
            if not is_first:
                flow[...] = grad_in
            part_mix[layer] = mix_part
            part_vec[layer, 0:1] = gain_part
            part_vec[layer, 1:2] = bias_part
            out1[layer, 0:half] = rows_of(part_mix, layer, (1 - core) * half, half)
            out1[layer, half:half_long] = part_vec[layer]

        def sum_cores(layer):
            mix_half = rows_of(part_mix, layer, core * half, half) + in1[layer, 0:half]
            vec_half = part_vec[layer] + in1[layer, half:half_long]
            for index in range(4):
                out2[index, layer, 0:eighth] = mix_half[index * eighth : (index + 1) * eighth]
                out2[index, layer, eighth:long] = vec_half

        def sum_pair(couple):
            exchange1(couple).wait_recv()
            sum_cores(2 * couple)
            sum_cores(2 * couple + 1)

        def to_chips(couple):
            for flip in (3, 2, 1):
                exchange2(couple, flip).start()

        def sum_chips(couples):
            for couple in couples:
                for flip in (1, 2, 3):
                    exchange2(couple, flip).wait_recv()
            group = [2 * couple + odd for couple in couples for odd in (0, 1)]
            for layer in group:
                in2[chip, layer, 0:long] = out2[chip, layer, 0:long]
            squares, vec_squares = 0.0, 0.0
            for layer in group:
                mix_sum, vec_sum = (
                    (in2[0, layer, rows] + in2[1, layer, rows])
                    + (in2[2, layer, rows] + in2[3, layer, rows])
                    for rows in (slice(0, eighth), slice(eighth, long))
                )
                out4[layer, 0:eighth] = mix_sum
                out4[layer, eighth:long] = vec_sum
                squares += mix_sum * mix_sum
                vec_squares += vec_sum * vec_sum
            square[0] += jnp.sum(squares, axis=0, keepdims=True) + (
                1.0 / lax.axis_size("dp")
            ) * jnp.sum(vec_squares, axis=0, keepdims=True)

        couples = layers // 2

        @pl.loop(0, LAG)
        def _(tick):
            couple = couples - 1 - tick
            back(2 * couple + 1)
            back(2 * couple)
            exchange1(couple).start()

        @pl.loop(LAG, couples - 1)
        def _(tick):
            couple = couples - 1 - tick
            sum_pair(couple + LAG)
            back(2 * couple + 1)
            to_chips(couple + LAG)
            back(2 * couple)
            exchange1(couple).start()

        back(1)
        back(0, True)
        exchange1(0).start()
        for couple in range(LAG, 0, -1):
            sum_pair(couple)
            to_chips(couple)
        sum_chips((6, 7))
        sum_pair(0)
        to_chips(0)
        sum_chips((4, 5))
        sum_chips((3, 2))
        sum_chips((1, 0))

    def column_place(step):
        to_column = lax.rem(column + lax.div(step, 4), 4)
        to_tp = lax.rem(tp + lax.rem(step, 4), 4)
        return to_column * 4 + to_tp, dict(section=x_place * 4 + to_column, tp=to_tp)

    def plane_place(step):
        to_x = lax.rem(x_place + lax.div(step, dps), sections // 4)
        to_dp = lax.rem(dp + lax.rem(step, dps), dps)
        return to_x * dps + to_dp, dict(section=to_x * 4 + column, dp=to_dp)

    def early_copies_left():
        for other_pair in range(pairs):
            item, goes, mine, to_dp, to_tp = x_plan(other_pair)

            @pl.when(goes & jnp.logical_not(mine))
            def _():
                columns = pl.ds(pl.multiple_of(item * size, size), size)
                remote(
                    x_ref.at[:, :, columns], x_in, x_sent.at[other_pair], x_came, tp=to_tp, dp=to_dp
                ).wait_send()

        @pl.loop(low, high_end)
        def _(to_unit):
            for bit in range(2):
                to_section = to_unit * 2 + bit
                for to_core in range(2):

                    @pl.when(jnp.logical_not((to_section == section) & (core == to_core)))
                    def _():
                        rows = pl.ds(to_core * half, half)
                        remote(
                            stage.at[0],
                            params.at[section],
                            p_sent.at[to_section, to_core],
                            p_came.at[section],
                            tp=sibling,
                        ).wait_send()
                        remote(
                            mix_ref.at[0, rows],
                            weights.at[section, rows],
                            w_sent.at[to_section, to_core],
                            w_came.at[section],
                            tp=sibling,
                        ).wait_send()

        @pl.when(active)
        def _():
            @pl.loop(0, layers)
            def _(layer):
                forward_half(layer).wait_send()

            @pl.loop(0, layers // 2)
            def _(couple):
                exchange1(couple).wait_send()
                for flip in (1, 2, 3):
                    exchange2(couple, flip).wait_send()

    def owner_copies_left():
        @pl.when(active)
        def _():
            @pl.loop(0, layers)
            def _(layer):
                @pl.when(jnp.logical_not(is_owner(layer)))
                def _():
                    to_owner(layer).wait_send()

    stages = (
        (column_place, all_column, column_sent, column_came),
        (plane_place, all_plane, plane_sent, plane_came),
    )
    for index, (place_of, slots, sent, came) in enumerate(stages):
        count = slots.shape[0]
        mine, _ = place_of(0)
        slots[mine] = square[index]

        def copy_to(step, index=index, place_of=place_of, slots=slots, sent=sent, came=came):
            place, where = place_of(step)
            here, _ = place_of(0)
            return remote(square.at[index], slots.at[here], sent.at[place], came.at[here], **where)

        def copy_from(step, index=index, place_of=place_of, slots=slots, sent=sent, came=came):
            place, where = place_of(step)
            return remote(square.at[index], slots.at[place], sent.at[place], came.at[place], **where)

        for step in range(1, count):
            copy_to(step).start()
        if index == 0:

            @pl.when(active)
            def _():
                @pl.loop(0, layers)
                def _(layer):
                    start_to_owner(lax.rem(layer + section, layers))

        if index == 0:
            early_copies_left()
        else:
            owner_copies_left()

        @pl.loop(1, count)
        def _(step):
            copy_to(step).wait_send()

        for step in range(1, count):
            copy_from(step).wait_recv()
        square[index + 1] = jnp.sum(slots[...], axis=0)

    total = jnp.sum(square[2], axis=-1, keepdims=True)
    scale = lax.rsqrt(total / param_count + GRAD_EPS)

    for item in range(heads):
        remote(
            out4.at[0, 0:long], in4.at[item, 0:long], sent4.at[0], came4.at[item], tp=sibling
        ).wait_recv()
        grads_ref[item, 0:long] = in4[item, 0:long] * scale


def shards(inputs, norm_gain, norm_bias, mix):
    sections, tps, replicas = (lax.axis_size(name) for name in ("section", "tp", "dp"))
    batches, block, features = inputs.shape
    heads, size = mix.shape[1], mix.shape[2]
    rows = batches * block
    param_count = sections * tps * (2 * features + heads * size * size)
    loss_scale = 1.0 / math.sqrt(rows * replicas)
    piece = size // 8 + 8
    f32, bf16 = jnp.float32, jnp.bfloat16
    dma = pltpu.SemaphoreType.DMA
    flops = 3 * 2 * sections * rows * size * size
    grads = pl.pallas_call(
        functools.partial(relay_kernel, loss_scale, float(param_count)),
        out_shape=jax.ShapeDtypeStruct((heads, piece, size), f32),
        in_specs=[
            pl.BlockSpec(memory_space=pl.ANY),
            pl.BlockSpec(memory_space=pl.ANY),
            pl.BlockSpec(memory_space=pl.ANY),
            pl.BlockSpec(memory_space=pl.ANY),
        ],
        out_specs=pl.BlockSpec(memory_space=pltpu.VMEM),
        scratch_shapes=[
            pltpu.VMEM((batches, block, size), bf16),
            pltpu.VMEM((2, 1, features), f32),
            pltpu.VMEM((heads, 2, size), f32),
            pltpu.VMEM((sections, 2, size), f32),
            pltpu.VMEM((sections, size, size), bf16),
            pltpu.VMEM((rows, size), bf16),
            pltpu.VMEM((sections, rows, size), f32),
            pltpu.VMEM((sections, rows, size), f32),
            pltpu.VMEM((sections, rows, size), bf16),
            pltpu.VMEM((sections, rows, size), f32),
            pltpu.VMEM((sections, size, size), f32),
            pltpu.VMEM((sections, 2, size), f32),
            pltpu.VMEM((sections, size // 2 + 8, size), f32),
            pltpu.VMEM((4, sections, piece, size), f32),
            pltpu.VMEM((sections, piece, size), f32),
            pltpu.VMEM((sections, size // 2 + 8, size), f32),
            pltpu.VMEM((4, sections, piece, size), f32),
            pltpu.VMEM((heads, piece, size), f32),
            pltpu.VMEM((3, 1, size), f32),
            pltpu.VMEM((4 * tps, 1, size), f32),
            pltpu.VMEM((sections // 4 * replicas, 1, size), f32),
            dma((2,)),
            dma((replicas // 2,)),
            dma,
            dma((sections, 2)),
            dma((sections,)),
            dma((sections, 2)),
            dma((sections,)),
            dma((sections,)),
            dma((sections,)),
            dma((sections,)),
            dma((sections // 2, 3)),
            dma((sections,)),
            dma((sections,)),
            dma((sections // 2, 3)),
            dma((heads,)),
            dma((4 * tps,)),
            dma((4 * tps,)),
            dma((sections // 4 * replicas,)),
            dma((sections // 4 * replicas,)),
        ],
        compiler_params=pltpu.CompilerParams(
            vmem_limit_bytes=60 << 20, collective_id=0, has_side_effects=True
        ),
        cost_estimate=pl.CostEstimate(
            flops=flops, bytes_accessed=4 << 20, transcendentals=sections * rows * size
        ),
        name="relay",
    )(inputs, norm_gain, norm_bias, mix[0])
    return (
        grads[:, size // 8].reshape(1, features),
        grads[:, size // 8 + 1].reshape(1, features),
        grads[None, :, : size // 8],
    )


def solution(mesh):
    placed = (
        P(None, "dp", "tp"),
        P("section", "tp"),
        P("section", "tp"),
        P("section", "tp", None, None),
    )
    return jax.shard_map(
        shards,
        mesh=mesh,
        in_specs=placed,
        out_specs=(P("section", "tp"), P("section", "tp"), P("section", "tp", "dp", None)),
        check_vma=False,
    )
```

```python
import functools
import math

import jax
import jax.numpy as jnp
from jax import lax
from jax.experimental import pallas as pl
from jax.experimental.pallas import tpu as pltpu
from jax.sharding import PartitionSpec as P

EPSILON = 1e-05
GRAD_EPS = 1e-06
GELU_K = math.sqrt(2.0 / math.pi)
GELU_C = 0.044715


def forward_layer(wide, gain, bias, weights):
    mean = jnp.mean(wide, axis=-1, keepdims=True)
    centred = wide - mean
    inv_std = lax.rsqrt(jnp.mean(centred * centred, axis=-1, keepdims=True) + EPSILON)
    normed = centred * inv_std
    pre = normed * gain + bias
    square = pre * pre
    tangent = jnp.tanh(pre * (GELU_K + (GELU_K * GELU_C) * square))
    half = 0.5 + 0.5 * tangent
    act = pre * half
    slope = half + act * (1.0 - tangent) * (GELU_K + (3.0 * GELU_K * GELU_C) * square)
    act = act.astype(jnp.bfloat16)
    mixed = jnp.dot(act, weights, preferred_element_type=jnp.float32)
    return (wide + mixed).astype(jnp.bfloat16), normed, inv_std, act, slope


def backward_layer(grad, normed, inv_std, act, slope, gain, weights, is_first):
    grad_act = lax.dot_general(
        grad, weights, (((1,), (1,)), ((), ())), preferred_element_type=jnp.float32
    )
    mix_part = lax.dot_general(
        act, grad, (((0,), (0,)), ((), ())), preferred_element_type=jnp.float32
    )
    grad_pre = grad_act * slope
    gain_term = grad_pre * normed
    gain_part = jnp.sum(gain_term, axis=0, keepdims=True)
    bias_part = jnp.sum(grad_pre, axis=0, keepdims=True)
    if is_first:
        return None, mix_part, gain_part, bias_part
    grad_norm = grad_pre * gain
    first = jnp.mean(grad_norm, axis=-1, keepdims=True)
    second = jnp.mean(gain_term * gain, axis=-1, keepdims=True)
    grad_in = grad.astype(jnp.float32) + inv_std * (grad_norm - first - normed * second)
    return grad_in.astype(jnp.bfloat16), mix_part, gain_part, bias_part


MESH = pl.DeviceIdType.MESH
LAG = 2
AHEAD = 4


def relay_kernel(
    loss_scale,
    param_count,
    x_ref,
    gain_ref,
    bias_ref,
    mix_ref,
    grads_ref,
    x_in,
    rows_in,
    stage,
    params,
    weights,
    flow,
    normed_s,
    inv_s,
    act_s,
    slope_s,
    part_mix,
    part_vec,
    out1,
    out2,
    out4,
    in1,
    in2,
    in4,
    square,
    all_column,
    all_plane,
    rows_came,
    x_sent,
    x_came,
    w_sent,
    w_came,
    p_sent,
    p_came,
    f_sent,
    f_came,
    sent1,
    sent2,
    sent4,
    came1,
    came2,
    came4,
    column_sent,
    column_came,
    plane_sent,
    plane_came,
):
    section, tp, dp = (lax.axis_index(name) for name in ("section", "tp", "dp"))
    layers = weights.shape[0]
    heads = mix_ref.shape[0]
    size = mix_ref.shape[1]
    half, eighth = size // 2, size // 8
    half_long, long = half + 2, eighth + 2
    pairs = lax.axis_size("dp") // 2
    core, high = lax.rem(tp, 2), lax.div(tp, 2)
    unit, z_bit = lax.div(section, 2), lax.rem(section, 2)
    pair, y_bit = lax.div(dp, 2), lax.rem(dp, 2)
    place = unit * pairs + pair
    kin = lax.div(place, heads)
    head = place - kin * heads
    active = place < 2 * heads
    owner_tp = high * 2 + kin
    part = core * 4 + y_bit * 2 + z_bit

    def remote(source, target, sent, came, **where):
        return pltpu.make_async_remote_copy(
            src_ref=source,
            dst_ref=target,
            send_sem=sent,
            recv_sem=came,
            device_id=where,
            device_id_type=MESH,
        )

    def send(is_here, source, target, sent, came, **where):
        @pl.when(is_here)
        def _():
            pltpu.make_async_copy(source, target, came).start()

        @pl.when(jnp.logical_not(is_here))
        def _():
            remote(source, target, sent, came, **where).start()

    for index, ref in enumerate((gain_ref, bias_ref)):
        pltpu.make_async_copy(ref, rows_in.at[index], rows_came.at[index]).start()
    sections, dps = lax.axis_size("section"), lax.axis_size("dp")
    column, x_place = lax.rem(section, 4), lax.div(section, 4)
    barrier = pltpu.get_barrier_semaphore()

    def greet(**where):
        pl.semaphore_signal(barrier, inc=1, device_id=where, device_id_type=MESH)

    greeted = 0
    for x_step in range(1, sections // 4):
        for step in range(1, dps):
            greet(
                section=lax.rem(x_place + x_step, sections // 4) * 4 + column,
                dp=lax.rem(dp + step, dps),
            )
            greeted += 1
    for step in range(4):
        for to_core in range(2):
            greet(section=x_place * 4 + step, tp=(1 - high) * 2 + to_core)
            greeted += 1
    for step in range(1, sections):
        for to_core in range(2):
            greet(section=lax.rem(section + step, sections), tp=high * 2 + to_core)
            greeted += 1
    for step in range(1, dps):
        for to_core in range(2):
            greet(dp=lax.rem(dp + step, dps), tp=high * 2 + to_core)
            greeted += 1
    greet(section=unit * 2 + 1 - z_bit, dp=pair * 2 + 1 - y_bit)
    greet(tp=high * 2 + 1 - core)
    greeted += 2
    square[...] = jnp.zeros_like(square)
    for index, ref in enumerate((gain_ref, bias_ref)):
        pltpu.make_async_copy(ref, rows_in.at[index], rows_came.at[index]).wait()
        for item in range(heads):
            columns = slice(item * size, (item + 1) * size)
            stage[item, index : index + 1] = rows_in[index, 0:1, columns]
    pl.semaphore_wait(barrier, greeted)

    def x_plan(other_pair):
        here = unit * pairs + other_pair
        goes = (lax.div(here, heads) == core) & (y_bit == z_bit)
        to_dp = other_pair * 2 + lax.rem(pair, 2)
        to_core = lax.div(dp, 4)
        mine = (to_dp == dp) & (to_core == core)
        return here - core * heads, goes, mine, to_dp, high * 2 + to_core

    for other_pair in range(pairs):
        item, goes, mine, to_dp, to_tp = x_plan(other_pair)

        @pl.when(goes)
        def _():
            columns = pl.ds(pl.multiple_of(item * size, size), size)
            send(
                mine,
                x_ref.at[:, :, columns],
                x_in,
                x_sent.at[other_pair],
                x_came,
                tp=to_tp,
                dp=to_dp,
            )

    middle = lax.div(heads + pairs - 1 - pair, pairs)
    stop = lax.div(2 * heads + pairs - 1 - pair, pairs)
    low = jnp.where(core == 0, 0, middle)
    high_end = jnp.where(core == 0, middle, stop)

    @pl.loop(0, high_end - low)
    def _(turn):
        to_unit = low + lax.rem(turn + unit, high_end - low)
        item = to_unit * pairs + pair - core * heads
        for bit in range(2):
            to_section = to_unit * 2 + bit
            for to_core in range(2):
                mine = (to_section == section) & (core == to_core)
                rows = pl.ds(to_core * half, half)
                to_tp = high * 2 + to_core
                send(
                    mine,
                    stage.at[item],
                    params.at[section],
                    p_sent.at[to_section, to_core],
                    p_came.at[section],
                    section=to_section,
                    tp=to_tp,
                )
                send(
                    mine,
                    mix_ref.at[item, rows],
                    weights.at[section, rows],
                    w_sent.at[to_section, to_core],
                    w_came.at[section],
                    section=to_section,
                    tp=to_tp,
                )

    sibling = high * 2 + 1 - core
    own_rows = pl.ds(pl.multiple_of(core * half, half), half)
    other_rows = pl.ds(pl.multiple_of((1 - core) * half, half), half)

    def forward_half(layer):
        own = weights.at[layer, own_rows]
        return remote(own, own, f_sent.at[layer], f_came.at[layer], tp=sibling)

    def pass_on(layer):
        own = weights.at[layer, own_rows]
        remote(own, own, w_sent.at[0, 0], w_came.at[layer], tp=sibling).wait_recv()
        forward_half(layer).start()

    def both(couple):
        return pl.ds(2 * couple, 2)

    def exchange1(couple):
        return remote(
            out1.at[both(couple), 0:half_long],
            in1.at[both(couple), 0:half_long],
            sent1.at[couple],
            came1.at[couple],
            tp=sibling,
        )

    chip = y_bit * 2 + z_bit

    def exchange2(couple, flip):
        to_y = lax.rem(y_bit + flip // 2, 2)
        to_z = lax.rem(z_bit + flip % 2, 2)
        return remote(
            out2.at[to_y * 2 + to_z, both(couple), 0:long],
            in2.at[chip, both(couple), 0:long],
            sent2.at[couple, flip - 1],
            came2.at[couple, flip - 1],
            section=unit * 2 + to_z,
            dp=pair * 2 + to_y,
        )

    def to_owner(layer):
        return remote(
            out4.at[layer, 0:long],
            in4.at[head, 0:long],
            sent4.at[layer],
            came4.at[head],
            section=layer,
            tp=owner_tp,
            dp=part,
        )

    def is_owner(layer):
        return (layer == section) & (owner_tp == tp) & (part == dp)

    def start_to_owner(layer):
        @pl.when(is_owner(layer))
        def _():
            pltpu.make_async_copy(
                out4.at[layer, 0:long], in4.at[head, 0:long], came4.at[head]
            ).start()

        @pl.when(jnp.logical_not(is_owner(layer)))
        def _():
            to_owner(layer).start()

    def rows_of(ref, layer, start, count):
        return ref[layer, pl.ds(pl.multiple_of(start, 8), count)]

    @pl.when(active)
    def _():
        remote(x_in, x_in, x_sent.at[0], x_came, tp=sibling).wait_recv()
        flow[...] = x_in[...].reshape(flow.shape)
        for layer in range(AHEAD):
            pass_on(layer)

        @pl.loop(0, layers)
        def _(layer):
            @pl.when(layer + AHEAD < layers)
            def _():
                pass_on(layer + AHEAD)

            remote(
                stage.at[0], params.at[layer], p_sent.at[0, 0], p_came.at[layer], tp=sibling
            ).wait_recv()
            theirs = weights.at[layer, other_rows]
            remote(theirs, theirs, f_sent.at[layer], f_came.at[layer], tp=sibling).wait_recv()
            wide = flow[...].astype(jnp.float32)
            out, normed, inv_std, act, slope = forward_layer(
                wide, params[layer, 0:1], params[layer, 1:2], weights[layer]
            )
            flow[...] = out
            normed_s[layer] = normed
            inv_s[layer] = jnp.broadcast_to(inv_std, normed.shape)
            act_s[layer] = act
            slope_s[layer] = slope

        flow[...] = (flow[...].astype(jnp.float32) * loss_scale).astype(jnp.bfloat16)

        def back(layer, is_first=False):
            grad_in, mix_part, gain_part, bias_part = backward_layer(
                flow[...],
                normed_s[layer],
                inv_s[layer],
                act_s[layer],
                slope_s[layer],
                params[layer, 0:1],
                weights[layer],
                is_first,
            )
            if not is_first:
                flow[...] = grad_in
            part_mix[layer] = mix_part
            part_vec[layer, 0:1] = gain_part
            part_vec[layer, 1:2] = bias_part
            out1[layer, 0:half] = rows_of(part_mix, layer, (1 - core) * half, half)
            out1[layer, half:half_long] = part_vec[layer]

        def sum_cores(layer):
            mix_half = rows_of(part_mix, layer, core * half, half) + in1[layer, 0:half]
            vec_half = part_vec[layer] + in1[layer, half:half_long]
            for index in range(4):
                out2[index, layer, 0:eighth] = mix_half[index * eighth : (index + 1) * eighth]
                out2[index, layer, eighth:long] = vec_half

        def sum_pair(couple):
            exchange1(couple).wait_recv()
            sum_cores(2 * couple)
            sum_cores(2 * couple + 1)

        def to_chips(couple):
            for flip in (3, 2, 1):
                exchange2(couple, flip).start()

        def sum_chips(couples):
            for couple in couples:
                for flip in (1, 2, 3):
                    exchange2(couple, flip).wait_recv()
            group = [2 * couple + odd for couple in couples for odd in (0, 1)]
            for layer in group:
                in2[chip, layer, 0:long] = out2[chip, layer, 0:long]
            squares, vec_squares = 0.0, 0.0
            for layer in group:
                mix_sum, vec_sum = (
                    (in2[0, layer, rows] + in2[1, layer, rows])
                    + (in2[2, layer, rows] + in2[3, layer, rows])
                    for rows in (slice(0, eighth), slice(eighth, long))
                )
                out4[layer, 0:eighth] = mix_sum
                out4[layer, eighth:long] = vec_sum
                squares += mix_sum * mix_sum
                vec_squares += vec_sum * vec_sum
            square[0] += jnp.sum(squares, axis=0, keepdims=True) + (
                1.0 / lax.axis_size("dp")
            ) * jnp.sum(vec_squares, axis=0, keepdims=True)

        couples = layers // 2

        @pl.loop(0, LAG)
        def _(tick):
            couple = couples - 1 - tick
            back(2 * couple + 1)
            back(2 * couple)
            exchange1(couple).start()

        @pl.loop(LAG, couples - 1)
        def _(tick):
            couple = couples - 1 - tick
            sum_pair(couple + LAG)
            back(2 * couple + 1)
            to_chips(couple + LAG)
            back(2 * couple)
            exchange1(couple).start()

        back(1)
        back(0, True)
        exchange1(0).start()
        for couple in range(LAG, 0, -1):
            sum_pair(couple)
            to_chips(couple)
        sum_chips((6, 7))
        sum_pair(0)
        to_chips(0)
        sum_chips((4, 5))
        sum_chips((3, 2))
        sum_chips((1, 0))

    def column_place(step):
        to_column = lax.rem(column + lax.div(step, 4), 4)
        to_tp = lax.rem(tp + lax.rem(step, 4), 4)
        return to_column * 4 + to_tp, dict(section=x_place * 4 + to_column, tp=to_tp)

    def plane_place(step):
        to_x = lax.rem(x_place + lax.div(step, dps), sections // 4)
        to_dp = lax.rem(dp + lax.rem(step, dps), dps)
        return to_x * dps + to_dp, dict(section=to_x * 4 + column, dp=to_dp)

    def early_copies_left():
        for other_pair in range(pairs):
            item, goes, mine, to_dp, to_tp = x_plan(other_pair)

            @pl.when(goes & jnp.logical_not(mine))
            def _():
                columns = pl.ds(pl.multiple_of(item * size, size), size)
                remote(
                    x_ref.at[:, :, columns], x_in, x_sent.at[other_pair], x_came, tp=to_tp, dp=to_dp
                ).wait_send()

        @pl.loop(low, high_end)
        def _(to_unit):
            for bit in range(2):
                to_section = to_unit * 2 + bit
                for to_core in range(2):

                    @pl.when(jnp.logical_not((to_section == section) & (core == to_core)))
                    def _():
                        rows = pl.ds(to_core * half, half)
                        remote(
                            stage.at[0],
                            params.at[section],
                            p_sent.at[to_section, to_core],
                            p_came.at[section],
                            tp=sibling,
                        ).wait_send()
                        remote(
                            mix_ref.at[0, rows],
                            weights.at[section, rows],
                            w_sent.at[to_section, to_core],
                            w_came.at[section],
                            tp=sibling,
                        ).wait_send()

        @pl.when(active)
        def _():
            @pl.loop(0, layers)
            def _(layer):
                forward_half(layer).wait_send()

            @pl.loop(0, layers // 2)
            def _(couple):
                exchange1(couple).wait_send()
                for flip in (1, 2, 3):
                    exchange2(couple, flip).wait_send()

    def owner_copies_left():
        @pl.when(active)
        def _():
            @pl.loop(0, layers)
            def _(layer):
                @pl.when(jnp.logical_not(is_owner(layer)))
                def _():
                    to_owner(layer).wait_send()

    stages = (
        (column_place, all_column, column_sent, column_came),
        (plane_place, all_plane, plane_sent, plane_came),
    )
    for index, (place_of, slots, sent, came) in enumerate(stages):
        count = slots.shape[0]
        mine, _ = place_of(0)
        slots[mine] = square[index]

        def copy_to(step, index=index, place_of=place_of, slots=slots, sent=sent, came=came):
            place, where = place_of(step)
            here, _ = place_of(0)
            return remote(square.at[index], slots.at[here], sent.at[place], came.at[here], **where)

        def copy_from(step, index=index, place_of=place_of, slots=slots, sent=sent, came=came):
            place, where = place_of(step)
            return remote(square.at[index], slots.at[place], sent.at[place], came.at[place], **where)

        for step in range(1, count):
            copy_to(step).start()
        if index == 0:

            @pl.when(active)
            def _():
                @pl.loop(0, layers)
                def _(layer):
                    start_to_owner(lax.rem(layer + section, layers))

        if index == 0:
            early_copies_left()
        else:
            owner_copies_left()

        @pl.loop(1, count)
        def _(step):
            copy_to(step).wait_send()

        for step in range(1, count):
            copy_from(step).wait_recv()
        square[index + 1] = jnp.sum(slots[...], axis=0)

    total = jnp.sum(square[2], axis=-1, keepdims=True)
    scale = lax.rsqrt(total / param_count + GRAD_EPS)

    for item in range(heads):
        remote(
            out4.at[0, 0:long], in4.at[item, 0:long], sent4.at[0], came4.at[item], tp=sibling
        ).wait_recv()
        grads_ref[item, 0:long] = in4[item, 0:long] * scale


def shards(inputs, norm_gain, norm_bias, mix):
    sections, tps, replicas = (lax.axis_size(name) for name in ("section", "tp", "dp"))
    batches, block, features = inputs.shape
    heads, size = mix.shape[1], mix.shape[2]
    rows = batches * block
    param_count = sections * tps * (2 * features + heads * size * size)
    loss_scale = 1.0 / math.sqrt(rows * replicas)
    piece = size // 8 + 8
    f32, bf16 = jnp.float32, jnp.bfloat16
    dma = pltpu.SemaphoreType.DMA
    flops = 3 * 2 * sections * rows * size * size
    grads = pl.pallas_call(
        functools.partial(relay_kernel, loss_scale, float(param_count)),
        out_shape=jax.ShapeDtypeStruct((heads, piece, size), f32),
        in_specs=[
            pl.BlockSpec(memory_space=pl.ANY),
            pl.BlockSpec(memory_space=pl.ANY),
            pl.BlockSpec(memory_space=pl.ANY),
            pl.BlockSpec(memory_space=pl.ANY),
        ],
        out_specs=pl.BlockSpec(memory_space=pltpu.VMEM),
        scratch_shapes=[
            pltpu.VMEM((batches, block, size), bf16),
            pltpu.VMEM((2, 1, features), f32),
            pltpu.VMEM((heads, 2, size), f32),
            pltpu.VMEM((sections, 2, size), f32),
            pltpu.VMEM((sections, size, size), bf16),
            pltpu.VMEM((rows, size), bf16),
            pltpu.VMEM((sections, rows, size), f32),
            pltpu.VMEM((sections, rows, size), f32),
            pltpu.VMEM((sections, rows, size), bf16),
            pltpu.VMEM((sections, rows, size), f32),
            pltpu.VMEM((sections, size, size), f32),
            pltpu.VMEM((sections, 2, size), f32),
            pltpu.VMEM((sections, size // 2 + 8, size), f32),
            pltpu.VMEM((4, sections, piece, size), f32),
            pltpu.VMEM((sections, piece, size), f32),
            pltpu.VMEM((sections, size // 2 + 8, size), f32),
            pltpu.VMEM((4, sections, piece, size), f32),
            pltpu.VMEM((heads, piece, size), f32),
            pltpu.VMEM((3, 1, size), f32),
            pltpu.VMEM((4 * tps, 1, size), f32),
            pltpu.VMEM((sections // 4 * replicas, 1, size), f32),
            dma((2,)),
            dma((replicas // 2,)),
            dma,
            dma((sections, 2)),
            dma((sections,)),
            dma((sections, 2)),
            dma((sections,)),
            dma((sections,)),
            dma((sections,)),
            dma((sections,)),
            dma((sections // 2, 3)),
            dma((sections,)),
            dma((sections,)),
            dma((sections // 2, 3)),
            dma((heads,)),
            dma((4 * tps,)),
            dma((4 * tps,)),
            dma((sections // 4 * replicas,)),
            dma((sections // 4 * replicas,)),
        ],
        compiler_params=pltpu.CompilerParams(
            vmem_limit_bytes=60 << 20, collective_id=0, has_side_effects=True
        ),
        cost_estimate=pl.CostEstimate(
            flops=flops, bytes_accessed=4 << 20, transcendentals=sections * rows * size
        ),
        name="relay",
    )(inputs, norm_gain, norm_bias, mix[0])
    return (
        grads[:, size // 8].reshape(1, features),
        grads[:, size // 8 + 1].reshape(1, features),
        grads[None, :, : size // 8],
    )


def solution(mesh):
    placed = (
        P(None, "dp", "tp"),
        P("section", "tp"),
        P("section", "tp"),
        P("section", "tp", None, None),
    )
    return jax.shard_map(
        shards,
        mesh=mesh,
        in_specs=placed,
        out_specs=(P("section", "tp"), P("section", "tp"), P("section", "tp", "dp", None)),
        check_vma=False,
    )
```

```python
import functools
import math

import jax
import jax.numpy as jnp
from jax import lax
from jax.experimental import pallas as pl
from jax.experimental.pallas import tpu as pltpu
from jax.sharding import PartitionSpec as P

EPSILON = 1e-05
GRAD_EPS = 1e-06
GELU_K = math.sqrt(2.0 / math.pi)
GELU_C = 0.044715


def forward_layer(wide, gain, bias, weights):
    mean = jnp.mean(wide, axis=-1, keepdims=True)
    centred = wide - mean
    inv_std = lax.rsqrt(jnp.mean(centred * centred, axis=-1, keepdims=True) + EPSILON)
    normed = centred * inv_std
    pre = normed * gain + bias
    square = pre * pre
    tangent = jnp.tanh(pre * (GELU_K + (GELU_K * GELU_C) * square))
    half = 0.5 + 0.5 * tangent
    act = pre * half
    slope = half + act * (1.0 - tangent) * (GELU_K + (3.0 * GELU_K * GELU_C) * square)
    act = act.astype(jnp.bfloat16)
    mixed = jnp.dot(act, weights, preferred_element_type=jnp.float32)
    return (wide + mixed).astype(jnp.bfloat16), normed, inv_std, act, slope


def backward_layer(grad, normed, inv_std, act, slope, gain, weights, is_first):
    grad_act = lax.dot_general(
        grad, weights, (((1,), (1,)), ((), ())), preferred_element_type=jnp.float32
    )
    mix_part = lax.dot_general(
        act, grad, (((0,), (0,)), ((), ())), preferred_element_type=jnp.float32
    )
    grad_pre = grad_act * slope
    gain_term = grad_pre * normed
    gain_part = jnp.sum(gain_term, axis=0, keepdims=True)
    bias_part = jnp.sum(grad_pre, axis=0, keepdims=True)
    if is_first:
        return None, mix_part, gain_part, bias_part
    grad_norm = grad_pre * gain
    first = jnp.mean(grad_norm, axis=-1, keepdims=True)
    second = jnp.mean(gain_term * gain, axis=-1, keepdims=True)
    grad_in = grad.astype(jnp.float32) + inv_std * (grad_norm - first - normed * second)
    return grad_in.astype(jnp.bfloat16), mix_part, gain_part, bias_part


MESH = pl.DeviceIdType.MESH
LAG = 2
AHEAD = 4


def relay_kernel(
    loss_scale,
    param_count,
    x_ref,
    gain_ref,
    bias_ref,
    mix_ref,
    grads_ref,
    x_in,
    rows_in,
    stage,
    params,
    weights,
    flow,
    normed_s,
    inv_s,
    act_s,
    slope_s,
    part_mix,
    part_vec,
    out1,
    out2,
    out4,
    in1,
    in2,
    in4,
    square,
    all_column,
    all_plane,
    rows_came,
    x_sent,
    x_came,
    w_sent,
    w_came,
    p_sent,
    p_came,
    f_sent,
    f_came,
    sent1,
    sent2,
    sent4,
    came1,
    came2,
    came4,
    column_sent,
    column_came,
    plane_sent,
    plane_came,
):
    section, tp, dp = (lax.axis_index(name) for name in ("section", "tp", "dp"))
    layers = weights.shape[0]
    heads = mix_ref.shape[0]
    size = mix_ref.shape[1]
    half, eighth = size // 2, size // 8
    half_long, long = half + 2, eighth + 2
    pairs = lax.axis_size("dp") // 2
    core, high = lax.rem(tp, 2), lax.div(tp, 2)
    unit, z_bit = lax.div(section, 2), lax.rem(section, 2)
    pair, y_bit = lax.div(dp, 2), lax.rem(dp, 2)
    place = unit * pairs + pair
    kin = lax.div(place, heads)
    head = place - kin * heads
    active = place < 2 * heads
    owner_tp = high * 2 + kin
    part = core * 4 + y_bit * 2 + z_bit

    def remote(source, target, sent, came, **where):
        return pltpu.make_async_remote_copy(
            src_ref=source,
            dst_ref=target,
            send_sem=sent,
            recv_sem=came,
            device_id=where,
            device_id_type=MESH,
        )

    def send(is_here, source, target, sent, came, **where):
        @pl.when(is_here)
        def _():
            pltpu.make_async_copy(source, target, came).start()

        @pl.when(jnp.logical_not(is_here))
        def _():
            remote(source, target, sent, came, **where).start()

    for index, ref in enumerate((gain_ref, bias_ref)):
        pltpu.make_async_copy(ref, rows_in.at[index], rows_came.at[index]).start()
    sections, dps = lax.axis_size("section"), lax.axis_size("dp")
    column, x_place = lax.rem(section, 4), lax.div(section, 4)
    barrier = pltpu.get_barrier_semaphore()

    def greet(**where):
        pl.semaphore_signal(barrier, inc=1, device_id=where, device_id_type=MESH)

    greeted = 0
    for x_step in range(1, sections // 4):
        for step in range(1, dps):
            greet(
                section=lax.rem(x_place + x_step, sections // 4) * 4 + column,
                dp=lax.rem(dp + step, dps),
            )
            greeted += 1
    for step in range(4):
        for to_core in range(2):
            greet(section=x_place * 4 + step, tp=(1 - high) * 2 + to_core)
            greeted += 1
    for step in range(1, sections):
        for to_core in range(2):
            greet(section=lax.rem(section + step, sections), tp=high * 2 + to_core)
            greeted += 1
    for step in range(1, dps):
        for to_core in range(2):
            greet(dp=lax.rem(dp + step, dps), tp=high * 2 + to_core)
            greeted += 1
    greet(section=unit * 2 + 1 - z_bit, dp=pair * 2 + 1 - y_bit)
    greet(tp=high * 2 + 1 - core)
    greeted += 2
    square[...] = jnp.zeros_like(square)
    pl.semaphore_wait(barrier, greeted)

    def x_plan(other_pair):
        here = unit * pairs + other_pair
        goes = (lax.div(here, heads) == core) & (y_bit == z_bit)
        to_dp = other_pair * 2 + lax.rem(pair, 2)
        to_core = lax.div(dp, 4)
        mine = (to_dp == dp) & (to_core == core)
        return here - core * heads, goes, mine, to_dp, high * 2 + to_core

    for other_pair in range(pairs):
        item, goes, mine, to_dp, to_tp = x_plan(other_pair)

        @pl.when(goes)
        def _():
            columns = pl.ds(pl.multiple_of(item * size, size), size)
            send(
                mine,
                x_ref.at[:, :, columns],
                x_in,
                x_sent.at[other_pair],
                x_came,
                tp=to_tp,
                dp=to_dp,
            )

    for index, ref in enumerate((gain_ref, bias_ref)):
        pltpu.make_async_copy(ref, rows_in.at[index], rows_came.at[index]).wait()
        for item in range(heads):
            columns = slice(item * size, (item + 1) * size)
            stage[item, index : index + 1] = rows_in[index, 0:1, columns]
    middle = lax.div(heads + pairs - 1 - pair, pairs)
    stop = lax.div(2 * heads + pairs - 1 - pair, pairs)
    low = jnp.where(core == 0, 0, middle)
    high_end = jnp.where(core == 0, middle, stop)

    @pl.loop(0, high_end - low)
    def _(turn):
        to_unit = low + lax.rem(turn + unit, high_end - low)
        item = to_unit * pairs + pair - core * heads
        for bit in range(2):
            to_section = to_unit * 2 + bit
            for to_core in range(2):
                mine = (to_section == section) & (core == to_core)
                rows = pl.ds(to_core * half, half)
                to_tp = high * 2 + to_core
                send(
                    mine,
                    stage.at[item],
                    params.at[section],
                    p_sent.at[to_section, to_core],
                    p_came.at[section],
                    section=to_section,
                    tp=to_tp,
                )
                send(
                    mine,
                    mix_ref.at[item, rows],
                    weights.at[section, rows],
                    w_sent.at[to_section, to_core],
                    w_came.at[section],
                    section=to_section,
                    tp=to_tp,
                )

    sibling = high * 2 + 1 - core
    own_rows = pl.ds(pl.multiple_of(core * half, half), half)
    other_rows = pl.ds(pl.multiple_of((1 - core) * half, half), half)

    def forward_half(layer):
        own = weights.at[layer, own_rows]
        return remote(own, own, f_sent.at[layer], f_came.at[layer], tp=sibling)

    def pass_on(layer):
        own = weights.at[layer, own_rows]
        remote(own, own, w_sent.at[0, 0], w_came.at[layer], tp=sibling).wait_recv()
        forward_half(layer).start()

    def both(couple):
        return pl.ds(2 * couple, 2)

    def exchange1(couple):
        return remote(
            out1.at[both(couple), 0:half_long],
            in1.at[both(couple), 0:half_long],
            sent1.at[couple],
            came1.at[couple],
            tp=sibling,
        )

    chip = y_bit * 2 + z_bit

    def exchange2(couple, flip):
        to_y = lax.rem(y_bit + flip // 2, 2)
        to_z = lax.rem(z_bit + flip % 2, 2)
        return remote(
            out2.at[to_y * 2 + to_z, both(couple), 0:long],
            in2.at[chip, both(couple), 0:long],
            sent2.at[couple, flip - 1],
            came2.at[couple, flip - 1],
            section=unit * 2 + to_z,
            dp=pair * 2 + to_y,
        )

    def to_owner(layer):
        return remote(
            out4.at[layer, 0:long],
            in4.at[head, 0:long],
            sent4.at[layer],
            came4.at[head],
            section=layer,
            tp=owner_tp,
            dp=part,
        )

    def is_owner(layer):
        return (layer == section) & (owner_tp == tp) & (part == dp)

    def start_to_owner(layer):
        @pl.when(is_owner(layer))
        def _():
            pltpu.make_async_copy(
                out4.at[layer, 0:long], in4.at[head, 0:long], came4.at[head]
            ).start()

        @pl.when(jnp.logical_not(is_owner(layer)))
        def _():
            to_owner(layer).start()

    def rows_of(ref, layer, start, count):
        return ref[layer, pl.ds(pl.multiple_of(start, 8), count)]

    @pl.when(active)
    def _():
        remote(x_in, x_in, x_sent.at[0], x_came, tp=sibling).wait_recv()
        flow[...] = x_in[...].reshape(flow.shape)
        for layer in range(AHEAD):
            pass_on(layer)

        @pl.loop(0, layers)
        def _(layer):
            @pl.when(layer + AHEAD < layers)
            def _():
                pass_on(layer + AHEAD)

            remote(
                stage.at[0], params.at[layer], p_sent.at[0, 0], p_came.at[layer], tp=sibling
            ).wait_recv()
            theirs = weights.at[layer, other_rows]
            remote(theirs, theirs, f_sent.at[layer], f_came.at[layer], tp=sibling).wait_recv()
            wide = flow[...].astype(jnp.float32)
            out, normed, inv_std, act, slope = forward_layer(
                wide, params[layer, 0:1], params[layer, 1:2], weights[layer]
            )
            flow[...] = out
            normed_s[layer] = normed
            inv_s[layer] = jnp.broadcast_to(inv_std, normed.shape)
            act_s[layer] = act
            slope_s[layer] = slope

        flow[...] = (flow[...].astype(jnp.float32) * loss_scale).astype(jnp.bfloat16)

        def back(layer, is_first=False):
            grad_in, mix_part, gain_part, bias_part = backward_layer(
                flow[...],
                normed_s[layer],
                inv_s[layer],
                act_s[layer],
                slope_s[layer],
                params[layer, 0:1],
                weights[layer],
                is_first,
            )
            if not is_first:
                flow[...] = grad_in
            part_mix[layer] = mix_part
            part_vec[layer, 0:1] = gain_part
            part_vec[layer, 1:2] = bias_part
            out1[layer, 0:half] = rows_of(part_mix, layer, (1 - core) * half, half)
            out1[layer, half:half_long] = part_vec[layer]

        def sum_cores(layer):
            mix_half = rows_of(part_mix, layer, core * half, half) + in1[layer, 0:half]
            vec_half = part_vec[layer] + in1[layer, half:half_long]
            for index in range(4):
                out2[index, layer, 0:eighth] = mix_half[index * eighth : (index + 1) * eighth]
                out2[index, layer, eighth:long] = vec_half

        def sum_pair(couple):
            exchange1(couple).wait_recv()
            sum_cores(2 * couple)
            sum_cores(2 * couple + 1)

        def to_chips(couple):
            for flip in (3, 2, 1):
                exchange2(couple, flip).start()

        def sum_chips(couples):
            for couple in couples:
                for flip in (1, 2, 3):
                    exchange2(couple, flip).wait_recv()
            group = [2 * couple + odd for couple in couples for odd in (0, 1)]
            for layer in group:
                in2[chip, layer, 0:long] = out2[chip, layer, 0:long]
            squares, vec_squares = 0.0, 0.0
            for layer in group:
                mix_sum, vec_sum = (
                    (in2[0, layer, rows] + in2[1, layer, rows])
                    + (in2[2, layer, rows] + in2[3, layer, rows])
                    for rows in (slice(0, eighth), slice(eighth, long))
                )
                out4[layer, 0:eighth] = mix_sum
                out4[layer, eighth:long] = vec_sum
                squares += mix_sum * mix_sum
                vec_squares += vec_sum * vec_sum
            square[0] += jnp.sum(squares, axis=0, keepdims=True) + (
                1.0 / lax.axis_size("dp")
            ) * jnp.sum(vec_squares, axis=0, keepdims=True)

        couples = layers // 2

        @pl.loop(0, LAG)
        def _(tick):
            couple = couples - 1 - tick
            back(2 * couple + 1)
            back(2 * couple)
            exchange1(couple).start()

        @pl.loop(LAG, couples - 1)
        def _(tick):
            couple = couples - 1 - tick
            sum_pair(couple + LAG)
            back(2 * couple + 1)
            to_chips(couple + LAG)
            back(2 * couple)
            exchange1(couple).start()

        back(1)
        back(0, True)
        exchange1(0).start()
        for couple in range(LAG, 0, -1):
            sum_pair(couple)
            to_chips(couple)
        sum_pair(0)
        to_chips(0)
        sum_chips((6, 7))
        sum_chips((4, 5))
        sum_chips((3, 2))
        sum_chips((1, 0))

    def column_place(step):
        to_column = lax.rem(column + lax.div(step, 4), 4)
        to_tp = lax.rem(tp + lax.rem(step, 4), 4)
        return to_column * 4 + to_tp, dict(section=x_place * 4 + to_column, tp=to_tp)

    def plane_place(step):
        to_x = lax.rem(x_place + lax.div(step, dps), sections // 4)
        to_dp = lax.rem(dp + lax.rem(step, dps), dps)
        return to_x * dps + to_dp, dict(section=to_x * 4 + column, dp=to_dp)

    def early_copies_left():
        for other_pair in range(pairs):
            item, goes, mine, to_dp, to_tp = x_plan(other_pair)

            @pl.when(goes & jnp.logical_not(mine))
            def _():
                columns = pl.ds(pl.multiple_of(item * size, size), size)
                remote(
                    x_ref.at[:, :, columns], x_in, x_sent.at[other_pair], x_came, tp=to_tp, dp=to_dp
                ).wait_send()

        @pl.loop(low, high_end)
        def _(to_unit):
            for bit in range(2):
                to_section = to_unit * 2 + bit
                for to_core in range(2):

                    @pl.when(jnp.logical_not((to_section == section) & (core == to_core)))
                    def _():
                        rows = pl.ds(to_core * half, half)
                        remote(
                            stage.at[0],
                            params.at[section],
                            p_sent.at[to_section, to_core],
                            p_came.at[section],
                            tp=sibling,
                        ).wait_send()
                        remote(
                            mix_ref.at[0, rows],
                            weights.at[section, rows],
                            w_sent.at[to_section, to_core],
                            w_came.at[section],
                            tp=sibling,
                        ).wait_send()

        @pl.when(active)
        def _():
            @pl.loop(0, layers)
            def _(layer):
                forward_half(layer).wait_send()

            @pl.loop(0, layers // 2)
            def _(couple):
                exchange1(couple).wait_send()
                for flip in (1, 2, 3):
                    exchange2(couple, flip).wait_send()

    def owner_copies_left():
        @pl.when(active)
        def _():
            @pl.loop(0, layers)
            def _(layer):
                @pl.when(jnp.logical_not(is_owner(layer)))
                def _():
                    to_owner(layer).wait_send()

    stages = (
        (column_place, all_column, column_sent, column_came),
        (plane_place, all_plane, plane_sent, plane_came),
    )
    for index, (place_of, slots, sent, came) in enumerate(stages):
        count = slots.shape[0]
        mine, _ = place_of(0)
        slots[mine] = square[index]

        def copy_to(step, index=index, place_of=place_of, slots=slots, sent=sent, came=came):
            place, where = place_of(step)
            here, _ = place_of(0)
            return remote(square.at[index], slots.at[here], sent.at[place], came.at[here], **where)

        def copy_from(step, index=index, place_of=place_of, slots=slots, sent=sent, came=came):
            place, where = place_of(step)
            return remote(square.at[index], slots.at[place], sent.at[place], came.at[place], **where)

        for step in range(1, count):
            copy_to(step).start()
        if index == 0:

            @pl.when(active)
            def _():
                @pl.loop(0, layers)
                def _(layer):
                    start_to_owner(lax.rem(layer + section, layers))

        if index == 0:
            early_copies_left()
        else:
            owner_copies_left()

        @pl.loop(1, count)
        def _(step):
            copy_to(step).wait_send()

        for step in range(1, count):
            copy_from(step).wait_recv()
        square[index + 1] = jnp.sum(slots[...], axis=0)

    total = jnp.sum(square[2], axis=-1, keepdims=True)
    scale = lax.rsqrt(total / param_count + GRAD_EPS)

    for item in range(heads):
        remote(
            out4.at[0, 0:long], in4.at[item, 0:long], sent4.at[0], came4.at[item], tp=sibling
        ).wait_recv()
        grads_ref[item, 0:long] = in4[item, 0:long] * scale


def shards(inputs, norm_gain, norm_bias, mix):
    sections, tps, replicas = (lax.axis_size(name) for name in ("section", "tp", "dp"))
    batches, block, features = inputs.shape
    heads, size = mix.shape[1], mix.shape[2]
    rows = batches * block
    param_count = sections * tps * (2 * features + heads * size * size)
    loss_scale = 1.0 / math.sqrt(rows * replicas)
    piece = size // 8 + 8
    f32, bf16 = jnp.float32, jnp.bfloat16
    dma = pltpu.SemaphoreType.DMA
    flops = 3 * 2 * sections * rows * size * size
    grads = pl.pallas_call(
        functools.partial(relay_kernel, loss_scale, float(param_count)),
        out_shape=jax.ShapeDtypeStruct((heads, piece, size), f32),
        in_specs=[
            pl.BlockSpec(memory_space=pl.ANY),
            pl.BlockSpec(memory_space=pl.ANY),
            pl.BlockSpec(memory_space=pl.ANY),
            pl.BlockSpec(memory_space=pl.ANY),
        ],
        out_specs=pl.BlockSpec(memory_space=pltpu.VMEM),
        scratch_shapes=[
            pltpu.VMEM((batches, block, size), bf16),
            pltpu.VMEM((2, 1, features), f32),
            pltpu.VMEM((heads, 2, size), f32),
            pltpu.VMEM((sections, 2, size), f32),
            pltpu.VMEM((sections, size, size), bf16),
            pltpu.VMEM((rows, size), bf16),
            pltpu.VMEM((sections, rows, size), f32),
            pltpu.VMEM((sections, rows, size), f32),
            pltpu.VMEM((sections, rows, size), bf16),
            pltpu.VMEM((sections, rows, size), f32),
            pltpu.VMEM((sections, size, size), f32),
            pltpu.VMEM((sections, 2, size), f32),
            pltpu.VMEM((sections, size // 2 + 8, size), f32),
            pltpu.VMEM((4, sections, piece, size), f32),
            pltpu.VMEM((sections, piece, size), f32),
            pltpu.VMEM((sections, size // 2 + 8, size), f32),
            pltpu.VMEM((4, sections, piece, size), f32),
            pltpu.VMEM((heads, piece, size), f32),
            pltpu.VMEM((3, 1, size), f32),
            pltpu.VMEM((4 * tps, 1, size), f32),
            pltpu.VMEM((sections // 4 * replicas, 1, size), f32),
            dma((2,)),
            dma((replicas // 2,)),
            dma,
            dma((sections, 2)),
            dma((sections,)),
            dma((sections, 2)),
            dma((sections,)),
            dma((sections,)),
            dma((sections,)),
            dma((sections,)),
            dma((sections // 2, 3)),
            dma((sections,)),
            dma((sections,)),
            dma((sections // 2, 3)),
            dma((heads,)),
            dma((4 * tps,)),
            dma((4 * tps,)),
            dma((sections // 4 * replicas,)),
            dma((sections // 4 * replicas,)),
        ],
        compiler_params=pltpu.CompilerParams(
            vmem_limit_bytes=60 << 20, collective_id=0, has_side_effects=True
        ),
        cost_estimate=pl.CostEstimate(
            flops=flops, bytes_accessed=4 << 20, transcendentals=sections * rows * size
        ),
        name="relay",
    )(inputs, norm_gain, norm_bias, mix[0])
    return (
        grads[:, size // 8].reshape(1, features),
        grads[:, size // 8 + 1].reshape(1, features),
        grads[None, :, : size // 8],
    )


def solution(mesh):
    placed = (
        P(None, "dp", "tp"),
        P("section", "tp"),
        P("section", "tp"),
        P("section", "tp", None, None),
    )
    return jax.shard_map(
        shards,
        mesh=mesh,
        in_specs=placed,
        out_specs=(P("section", "tp"), P("section", "tp"), P("section", "tp", "dp", None)),
        check_vma=False,
    )
```
